128 devices in a mesh: row: 8 (over x_lo, y), col: 16 (over x_hi, z, core).
Axes of the slice: x: 4 (x_hi: 2, x_lo: 2; x = x_hi * 2 + x_lo), y: 4, z: 4, core: 2. Of those that a mesh axis runs over, the one named last changes fastest.
Arguments:
- inverse: bfloat16 [26624, 26624], P('row', 'col'), may hold values from -6 to 6
- panels: bfloat16 [2, 8192, 512], P(None, 'col'), may hold values from -0.0625 to 0.0625
- block_slot: int32 [208], replicated, may hold values from 0 to 207, as said below
- list_ids: int32 [2, 64], replicated, may hold values from 0 to 207, as said below
Outputs:
- packed_panels: float32 [2, 16384, 512], P(None, ('row', 'col'))
- diag_update: float32 [2, 512, 512], replicated
The draws below stay inside these ranges and needn't reach their ends.
Inputs may be any that keep to these rules, and one draw needn't show every extreme that they name: block_slot is a permutation of the slots. `list_ids`: each supernode lists distinct blocks; at most 16 of a supernode's listed blocks have slots in one grid row (slot // 26 equal), and in every supernode some grid row holds exactly 16. `list_ids`: in each aligned group of 4 list positions of a supernode, at most 1 listed blocks have slots in one grid column (slot // 13 equal).
All inputs are finite; a program needn't handle non-finite values.
Results may differ from the reference program's by a relative error of at most 0.0003.
Values may be sent and summed in bfloat16 or wider, within the bound.
A program may use at most 128 MiB of HBM per device.

```python
import jax
import jax.numpy as jnp
from jax import lax

ORDER = 26624
BS = 128
W = 512
SUPER = 2
LIST = 64
NBLK = 208
RB = 26
CB = 13
MAXR = 16
N_ROW = 8
N_COL = 16


def make_lists(key):
    perm = jax.random.permutation(jax.random.fold_in(key, 11), NBLK).astype(jnp.int32)
    inverse_perm = jnp.argsort(perm).astype(jnp.int32)
    grid_rows = NBLK // RB
    spare = LIST - MAXR
    base_count = spare // (grid_rows - 1)
    extra_count = spare % (grid_rows - 1)
    ranks = jnp.arange(grid_rows, dtype=jnp.int32)
    by_rank = jnp.where(ranks == 0, MAXR, base_count + jnp.where(ranks - 1 < extra_count, 1, 0)).astype(jnp.int32)
    lists = []
    for supernode in range(SUPER):
        super_key = jax.random.fold_in(key, 100 + supernode)
        row_perm = jax.random.permutation(jax.random.fold_in(super_key, 1), grid_rows)
        counts = jnp.zeros((grid_rows,), jnp.int32).at[row_perm].set(by_rank)
        row_keys = jax.random.split(jax.random.fold_in(super_key, 2), grid_rows)
        local_perm = jax.vmap(lambda one_key: jax.random.permutation(one_key, RB))(row_keys).astype(jnp.int32)
        within = jnp.arange(RB, dtype=jnp.int32)[None, :] < counts[:, None]
        slot_grid = jnp.arange(grid_rows, dtype=jnp.int32)[:, None] * RB + local_perm
        scores = jax.random.permutation(jax.random.fold_in(super_key, 3), grid_rows * RB).astype(jnp.int32)
        keyed = jnp.where(within.reshape(-1), scores, grid_rows * RB + scores)
        picked = jnp.argsort(keyed, stable=True)[:LIST]
        chosen_slots = slot_grid.reshape(-1)[picked].astype(jnp.int32)
        col_of = (chosen_slots // CB).astype(jnp.int32)
        order_scores = jax.random.permutation(jax.random.fold_in(super_key, 4), LIST).astype(jnp.int32)
        ordered = chosen_slots[jnp.argsort(col_of * LIST + order_scores, stable=True)]
        first_col = (ordered[0] // CB).astype(jnp.int32)
        grid_cols = NBLK // CB
        shift_by = (first_col + grid_cols // 2) % grid_cols
        index = jnp.arange(LIST, dtype=jnp.int32)
        target = (index + shift_by) % N_COL * (LIST // N_COL) + index // N_COL
        placed = jnp.zeros((LIST,), jnp.int32).at[target].set(ordered)
        lists.append(inverse_perm[placed])
    return (perm, jnp.stack(lists).astype(jnp.int32))


def draw_block_slot(key, part):
    return make_lists(key)[0]


def draw_list_ids(key, part):
    return make_lists(key)[1]


def shard_levels(rng, shape, cuts, least, high):
    level = 1.0
    for position, blocks in cuts:
        steps = jax.random.uniform(jax.random.fold_in(jax.random.fold_in(rng, 6), position), (blocks,), jnp.float32, least / len(cuts), high / len(cuts))
        level = level * jnp.repeat(jnp.exp(steps), shape[position] // blocks).reshape((-1,) + (1,) * (len(shape) - 1 - position))
    return level


def gaussian(own_key, shape, spread, bound, cuts=(), held_as=jnp.bfloat16):
    result = spread * jax.random.normal(own_key, shape, jnp.float32)
    if cuts:
        result = result * shard_levels(own_key, shape, cuts, -0.22, 0.18)
    return jnp.clip(result, -bound, bound).astype(held_as)


def setup_inputs(seed: int = 0) -> dict:
    key_of = jax.random.split(jax.random.key(seed), 5)
    return {
        "inverse": gaussian(key_of[0], (ORDER, ORDER), 1.0, 6.0, ((0, 8), (1, 16))),
        "panels": gaussian(key_of[1], (SUPER, LIST * BS, W), (LIST * BS) ** -0.5, 0.0625, ((1, 16),)),
        "block_slot": draw_block_slot(jax.random.fold_in(key_of[4], 71), 0),
        "list_ids": draw_list_ids(jax.random.fold_in(key_of[4], 71), 0),
    }


def reference(inverse, panels, block_slot, list_ids):
    blocked = inverse.reshape(NBLK, BS, NBLK, BS)
    packed_all = []
    diag_all = []
    positions = jnp.arange(LIST, dtype=jnp.int32)
    for supernode in range(SUPER):
        slots = block_slot[list_ids[supernode]].astype(jnp.int32)
        picked = blocked[slots[:, None], :, slots[None, :], :]
        picked = jnp.transpose(picked, (0, 2, 1, 3)).reshape(LIST * BS, LIST * BS)
        sums = jnp.dot(picked, panels[supernode], preferred_element_type=jnp.float32)
        diag_terms = -jnp.dot(panels[supernode].astype(jnp.float32).T, sums, precision=lax.Precision.HIGHEST)
        grid_row = (slots // RB).astype(jnp.int32)
        sum_blocks = sums.reshape(LIST, BS, W)

        def pack_row(row_id):
            keyed = jnp.where(grid_row == row_id, positions, LIST + positions)
            chosen = jnp.argsort(keyed, stable=True)[:MAXR]
            is_valid = grid_row[chosen] == row_id
            return jnp.where(is_valid[:, None, None], sum_blocks[chosen], jnp.zeros((), jnp.float32))

        packed = jax.vmap(pack_row)(jnp.arange(N_ROW, dtype=jnp.int32)).reshape(N_ROW * MAXR * BS, W)
        packed_all.append(packed)
        diag_all.append(diag_terms)
    return jnp.stack(packed_all), jnp.stack(diag_all)
```

```python
import functools

import jax
import jax.numpy as jnp
from jax import lax
from jax.experimental import pallas as pl
from jax.experimental.pallas import tpu as pltpu
from jax.sharding import PartitionSpec as P

BS = 128
MESH = pl.DeviceIdType.MESH
F32 = jnp.float32
BF16 = jnp.bfloat16


def tables(block_slot, list_ids, n_rows, n_cols):
    n_blocks, listed = block_slot.shape[0], list_ids.shape[1]
    ids = jnp.arange(n_blocks, dtype=jnp.int32)
    slots = jnp.sum(jnp.where(list_ids[..., None] == ids, block_slot, 0), axis=-1)
    col_blocks, row_blocks = n_blocks // n_cols, n_blocks // n_rows
    col = slots // col_blocks
    row = slots // row_blocks
    pos = jnp.arange(listed, dtype=jnp.int32)
    before = pos[None, :] < pos[:, None]
    rank = jnp.sum(((col[:, :, None] == col[:, None, :]) & before).astype(jnp.int32), axis=-1)
    kth = jnp.sum(((row[:, :, None] == row[:, None, :]) & before).astype(jnp.int32), axis=-1)
    code = 1 + (slots * 16 + rank) * 64 + pos

    def listed_in(group, index, groups):
        to_group = group[:, None, None, :] == jnp.arange(groups, dtype=jnp.int32)[:, None, None]
        to_index = index[:, None, None, :] == jnp.arange(16, dtype=jnp.int32)[:, None]
        return jnp.sum(jnp.where(to_group & to_index, code[:, None, None, :], 0), axis=-1)

    by_col = listed_in(col, rank, n_cols)
    by_row = listed_in(row, kth, n_rows)
    col_code, row_code = jnp.maximum(by_col - 1, 0), jnp.maximum(by_row - 1, 0)
    shard = listed // n_cols
    col_table = jnp.stack([(by_col > 0).astype(jnp.int32), col_code % 64 // shard, col_code // 1024 % col_blocks])
    row_table = jnp.stack([(by_row > 0).astype(jnp.int32), row_code // 1024 % row_blocks])
    of_col = jnp.repeat(row_code, n_cols // n_rows, axis=1)
    here = jnp.repeat(by_row, n_cols // n_rows, axis=1) > 0
    here &= of_col // 1024 // col_blocks == jnp.arange(n_cols, dtype=jnp.int32)[:, None]
    left_table = jnp.stack([here.astype(jnp.int32), jnp.where(here, of_col // 64 % 16, 0)])
    return col, col_table, row_table, left_table


def kernel(
    n_rows, n_cols, x_his,
    inv_hbm, pan, cols, by_col, by_row, by_k,
    out, diag,
    a_all, a_pick, p_send, p_recv, ag_send, p_all, l_send, l_recv, m_send, left,
    part, core_recv, z_recv, x_recv, d_part, d_sib, d_row, d_row_in, d_col, d_col_in, e_piece, e_col, e_row,
    a_sem, p_ss, p_rs, ag_ss, ag_rs, l_ss, l_rs, m_ss, m_rs, c_ss, c_rs, z_ss, z_rs, x_ss, x_rs,
    ds_ss, ds_rs, dr_ss, dr_rs, dc_ss, dc_rs, ec_ss, ec_rs, er_ss, er_rs, es_ss, es_rs,
):
    supers = pan.shape[0]
    sub = BS // n_rows
    col_blocks = a_all.shape[0]
    shard = pan.shape[1] // BS
    width = pan.shape[2]
    chips = n_cols // 2
    zs = chips // x_his
    me_r, me_c = lax.axis_index("row"), lax.axis_index("col")
    core = lax.rem(me_c, 2)
    chip = me_c // 2
    x_hi, z = chip // zs, lax.rem(chip, zs)
    sibling = (me_r, me_c + 1 - 2 * core)

    def remote(src, dst, ss, rs, to):
        return pltpu.make_async_remote_copy(
            src_ref=src, dst_ref=dst, send_sem=ss, recv_sem=rs, device_id=to, device_id_type=MESH
        )

    def load_a(b):
        columns = pl.ds(pl.multiple_of(b * BS, BS), BS)
        return pltpu.make_async_copy(inv_hbm.at[:, :, columns], a_all.at[b], a_sem.at[b])

    @pl.loop(0, col_blocks)
    def _(b):
        load_a(b).start()

    barrier = pltpu.get_barrier_semaphore()

    @pl.loop(1, n_cols)
    def _(d):
        pl.semaphore_signal(barrier, inc=1, device_id=(me_r, lax.rem(me_c + d, n_cols)), device_id_type=MESH)

    @pl.loop(1, n_rows)
    def _(d):
        pl.semaphore_signal(barrier, inc=1, device_id=(lax.rem(me_r + d, n_rows), me_c), device_id_type=MESH)

    def pick_for(c, s):
        piece = jnp.zeros((sub, width), BF16)
        for q in range(shard):
            block = pan[s, pl.ds(pl.multiple_of(q * BS + me_r * sub, sub), sub), :]
            piece = jnp.where(cols[s, me_c * shard + q] == c, block, piece)
        return piece

    @pl.loop(1, n_cols)
    def _(d):
        for s in range(supers):
            p_send[d, s] = pick_for(lax.rem(me_c + d, n_cols), s)

    for s in range(supers):
        p_recv[me_c, s] = pick_for(me_c, s)

    pl.semaphore_wait(barrier, n_cols + n_rows - 2)

    def p_copy(d):
        return remote(p_send.at[d], p_recv.at[me_c], p_ss.at[d], p_rs.at[d], (me_r, lax.rem(me_c + d, n_cols)))

    def p_arrive(d):
        return remote(p_send.at[d], p_recv.at[lax.rem(me_c - d + n_cols, n_cols)], p_ss.at[d], p_rs.at[d], (me_r, lax.rem(me_c + d, n_cols)))

    @pl.loop(1, n_cols)
    def _(d):
        p_copy(d).start()

    @pl.loop(1, n_cols)
    def _(d):
        p_arrive(d).wait_recv()

    def ag_copy(s, d):
        return remote(ag_send.at[s], p_all.at[s, :, me_r], ag_ss.at[s, d], ag_rs.at[s, d], (lax.rem(me_r + d, n_rows), me_c))

    def ag_arrive(s, d):
        return remote(ag_send.at[s], p_all.at[s, :, lax.rem(me_r - d + n_rows, n_rows)], ag_ss.at[s, d], ag_rs.at[s, d], (lax.rem(me_r + d, n_rows), me_c))

    for s in range(supers):
        @pl.loop(0, col_blocks)
        def _(i, s=s):
            block = p_recv[by_col[1, s, me_c, i], s]
            block = jnp.where(by_col[0, s, me_c, i] == 1, block, jnp.zeros_like(block))
            ag_send[s, i] = block
            p_all[s, i, me_r] = block

        @pl.loop(1, n_rows)
        def _(d, s=s):
            ag_copy(s, d).start()

    def left_for(k, s):
        block = ag_send[s, by_k[1, s, me_c, k]]
        return jnp.where(by_k[0, s, me_c, k] == 1, block, jnp.zeros_like(block))

    def l_copy(d):
        return remote(l_send.at[d], l_recv.at[me_c], l_ss.at[d], l_rs.at[d], (me_r, lax.rem(me_c + d, n_cols)))

    def l_arrive(d):
        return remote(l_send.at[d], l_recv.at[lax.rem(me_c - d + n_cols, n_cols)], l_ss.at[d], l_rs.at[d], (me_r, lax.rem(me_c + d, n_cols)))

    for s in range(supers):
        l_recv[me_c, s] = left_for(me_c, s)

    @pl.loop(1, n_cols)
    def _(d):
        for s in range(supers):
            l_send[d, s] = left_for(lax.rem(me_c + d, n_cols), s)
        l_copy(d).start()

    def c_copy(s, h):
        return remote(part.at[s, 0, h], core_recv.at[s, h], c_ss.at[s, h], c_rs.at[s, h], sibling)

    def z_copy(s, h, d):
        to = (me_r, (x_hi * zs + lax.rem(z + d, zs)) * 2 + core)
        return remote(part.at[s, 1, h, lax.rem(z + d, zs)], z_recv.at[s, h, d], z_ss.at[s, h, d], z_rs.at[s, h, d], to)

    def products(s):
        @pl.loop(1, n_rows)
        def _(d):
            ag_arrive(s, d).wait_recv()

        if s == 0:
            @pl.loop(0, col_blocks)
            def _(b):
                load_a(b).wait()

        @pl.loop(0, 2 * x_his)
        def _(i):
            mine, h = i // x_his, lax.rem(i, x_his)
            for u in range(zs):
                k = 2 * (h * zs + u) + jnp.where(mine == 1, core, 1 - core)
                a_row = by_row[1, s, me_r, k]
                for b in range(col_blocks):
                    a_pick[u * BS : (u + 1) * BS, b * BS : (b + 1) * BS] = a_all[by_col[2, s, me_c, b], a_row]
            product = jnp.dot(a_pick[...], p_all[s].reshape(col_blocks * BS, width), preferred_element_type=F32)
            part[s, mine, h] = product.reshape(zs, BS, width)

            @pl.when(mine == 0)
            def _():
                c_copy(s, h).start()

        for h in range(x_his):
            c_copy(s, h).wait_recv()
            part[s, 1, h] = part[s, 1, h] + core_recv[s, h]
            for d in range(1, zs):
                z_copy(s, h, d).start()

    def m_copy(d):
        return remote(m_send.at[d], left.at[:, me_r], m_ss.at[d], m_rs.at[d], (lax.rem(me_r + d, n_rows), me_c))

    def m_arrive(d):
        return remote(m_send.at[d], left.at[:, lax.rem(me_r - d + n_rows, n_rows)], m_ss.at[d], m_rs.at[d], (lax.rem(me_r + d, n_rows), me_c))

    products(0)

    @pl.loop(1, n_cols)
    def _(d):
        l_arrive(d).wait_recv()

    left[:, me_r] = l_recv[2 * me_r] + l_recv[2 * me_r + 1]

    @pl.loop(1, n_rows)
    def _(d):
        g = lax.rem(me_r + d, n_rows)
        m_send[d] = l_recv[2 * g] + l_recv[2 * g + 1]
        m_copy(d).start()

    products(1)

    @pl.loop(1, n_rows)
    def _(d):
        m_arrive(d).wait_recv()

    def x_copy(s):
        to = (me_r, ((1 - x_hi) * zs + z) * 2 + core)
        return remote(part.at[s, 1, 1 - x_hi, z], x_recv.at[s], x_ss.at[s], x_rs.at[s], to)

    def over_z(s, h):
        total = part[s, 1, h, z]
        for d in range(1, zs):
            z_copy(s, h, d).wait_recv()
            total = total + z_recv[s, h, d]
        part[s, 1, h, z] = total

    half = width // 2
    piece = half // n_rows

    def ds_copy(s):
        there = pl.ds(pl.multiple_of((1 - core) * half, half), half)
        return remote(d_part.at[s, there], d_sib.at[s], ds_ss.at[s], ds_rs.at[s], sibling)

    def dr_copy(s, d):
        g = lax.rem(me_r + d, n_rows)
        return remote(d_row.at[s, g], d_row_in.at[s, d], dr_ss.at[s, d], dr_rs.at[s, d], (g, me_c))

    def chip_at(d):
        return lax.rem(chip + d, chips)

    def dc_copy(s, d):
        t = chip_at(d)
        return remote(d_col.at[s, t], d_col_in.at[s, d], dc_ss.at[s, d], dc_rs.at[s, d], (me_r, 2 * t + core))

    def ec_copy(s, d, source):
        return remote(e_piece.at[s], e_col.at[s, source], ec_ss.at[s, d], ec_rs.at[s, d], (me_r, 2 * chip_at(d) + core))

    def rows_of(r):
        return pl.ds(pl.multiple_of(core * half + r * piece, piece), piece)

    def er_copy(s, d, source):
        to = (lax.rem(me_r + d, n_rows), me_c)
        return remote(e_row.at[s], diag.at[s, rows_of(source)], er_ss.at[s, d], er_rs.at[s, d], to)

    def es_copy(s, half_of):
        there = pl.ds(pl.multiple_of(half_of * half, half), half)
        return remote(diag.at[s, there], diag.at[s, there], es_ss.at[s], es_rs.at[s], sibling)

    def finish_sums(s):
        x_copy(s).wait_recv()
        total = part[s, 1, x_hi, z] + x_recv[s]
        valid = by_row[0, s, me_r, me_c] == 1
        total = jnp.where(valid, total, jnp.zeros_like(total))
        out[s] = total
        high = total.astype(BF16)
        low = (total - high.astype(F32)).astype(BF16)
        block = left[s].reshape(BS, width)
        contract = functools.partial(
            lax.dot_general, dimension_numbers=(((0,), (0,)), ((), ())), preferred_element_type=F32
        )
        d_part[s] = -(contract(block, high) + contract(block, low))
        ds_copy(s).start()

    def over_cores(s):
        ds_copy(s).wait_recv()
        here = pl.ds(pl.multiple_of(core * half, half), half)
        total = d_part[s, here] + d_sib[s]
        d_row[s] = total.reshape(n_rows, piece, width)

        @pl.loop(1, n_rows)
        def _(d):
            dr_copy(s, d).start()

    def over_rows(s):
        total = d_row[s, me_r]
        for d in range(1, n_rows):
            dr_copy(s, d).wait_recv()
            total = total + d_row_in[s, d]
        for t in range(chips):
            d_col[s, t] = total[(t // 2) * 8 : (t // 2) * 8 + 8, (t % 2) * half : (t % 2) * half + half]

        @pl.loop(1, chips)
        def _(d):
            dc_copy(s, d).start()

    def over_chips(s):
        total = d_col[s, chip]
        for d in range(1, chips):
            dc_copy(s, d).wait_recv()
            total = total + d_col_in[s, d]
        e_piece[s] = total
        e_col[s, chip] = total

        @pl.loop(1, chips)
        def _(d):
            ec_copy(s, d, chip).start()

    def back_over_chips(s):
        @pl.loop(1, chips)
        def _(d):
            ec_copy(s, d, lax.rem(chip - d + chips, chips)).wait_recv()

        for t in range(chips):
            e_row[s, (t // 2) * 8 : (t // 2) * 8 + 8, (t % 2) * half : (t % 2) * half + half] = e_col[s, t]
        diag[s, rows_of(me_r)] = e_row[s]

        @pl.loop(1, n_rows)
        def _(d):
            er_copy(s, d, me_r).start()

    def back_over_rows(s):
        @pl.loop(1, n_rows)
        def _(d):
            er_copy(s, d, lax.rem(me_r - d + n_rows, n_rows)).wait_recv()

        es_copy(s, core).start()

    over_z(0, 1 - x_hi)
    x_copy(0).start()
    over_z(0, x_hi)
    finish_sums(0)
    over_cores(0)
    over_z(1, 1 - x_hi)
    x_copy(1).start()
    over_z(1, x_hi)
    over_rows(0)
    finish_sums(1)
    over_cores(1)
    over_chips(0)
    over_rows(1)
    back_over_chips(0)
    over_chips(1)
    back_over_rows(0)
    back_over_chips(1)
    back_over_rows(1)

    @pl.loop(1, n_cols)
    def _(d):
        p_copy(d).wait_send()
        l_copy(d).wait_send()

    @pl.loop(1, n_rows)
    def _(d):
        m_copy(d).wait_send()

    for s in range(supers):
        @pl.loop(1, n_rows)
        def _(d, s=s):
            ag_copy(s, d).wait_send()
            dr_copy(s, d).wait_send()
            er_copy(s, d, me_r).wait_send()

        @pl.loop(1, chips)
        def _(d, s=s):
            dc_copy(s, d).wait_send()
            ec_copy(s, d, chip).wait_send()

        for h in range(x_his):
            c_copy(s, h).wait_send()
            for d in range(1, zs):
                z_copy(s, h, d).wait_send()
        x_copy(s).wait_send()
        ds_copy(s).wait_send()
        es_copy(s, core).wait_send()
        es_copy(s, 1 - core).wait_recv()


def local(n_rows, n_cols, inverse, panels, block_slot, list_ids):
    supers, _, width = panels.shape
    col_blocks = inverse.shape[1] // BS
    sub = BS // n_rows
    x_his = 2
    chips = n_cols // 2
    zs = chips // x_his
    half = width // 2
    piece = half // n_rows
    lists = tables(block_slot, list_ids, n_rows, n_cols)
    blocks = inverse.reshape(-1, BS, inverse.shape[1])
    vmem = pl.BlockSpec(memory_space=pltpu.VMEM)
    smem = pl.BlockSpec(memory_space=pltpu.SMEM)
    dma = pltpu.SemaphoreType.DMA
    scratch = [
        pltpu.VMEM((col_blocks, blocks.shape[0], BS, BS), BF16),
        pltpu.VMEM((zs * BS, col_blocks * BS), BF16),
        pltpu.VMEM((n_cols, supers, sub, width), BF16),
        pltpu.VMEM((n_cols, supers, sub, width), BF16),
        pltpu.VMEM((supers, col_blocks, sub, width), BF16),
        pltpu.VMEM((supers, col_blocks, n_rows, sub, width), BF16),
        pltpu.VMEM((n_cols, supers, sub, width), BF16),
        pltpu.VMEM((n_cols, supers, sub, width), BF16),
        pltpu.VMEM((n_rows, supers, sub, width), BF16),
        pltpu.VMEM((supers, n_rows, sub, width), BF16),
        pltpu.VMEM((supers, 2, x_his, zs, BS, width), F32),
        pltpu.VMEM((supers, x_his, zs, BS, width), F32),
        pltpu.VMEM((supers, x_his, zs, BS, width), F32),
        pltpu.VMEM((supers, BS, width), F32),
        pltpu.VMEM((supers, width, width), F32),
        pltpu.VMEM((supers, half, width), F32),
        pltpu.VMEM((supers, n_rows, piece, width), F32),
        pltpu.VMEM((supers, n_rows, piece, width), F32),
        pltpu.VMEM((supers, chips, 8, half), F32),
        pltpu.VMEM((supers, chips, 8, half), F32),
        pltpu.VMEM((supers, 8, half), F32),
        pltpu.VMEM((supers, chips, 8, half), F32),
        pltpu.VMEM((supers, piece, width), F32),
        dma((col_blocks,)),
        dma((n_cols,)), dma((n_cols,)),
        dma((supers, n_rows)), dma((supers, n_rows)),
        dma((n_cols,)), dma((n_cols,)),
        dma((n_rows,)), dma((n_rows,)),
        dma((supers, x_his)), dma((supers, x_his)),
        dma((supers, x_his, zs)), dma((supers, x_his, zs)),
        dma((supers,)), dma((supers,)),
        dma((supers,)), dma((supers,)),
        dma((supers, n_rows)), dma((supers, n_rows)),
        dma((supers, chips)), dma((supers, chips)),
        dma((supers, chips)), dma((supers, chips)),
        dma((supers, n_rows)), dma((supers, n_rows)),
        dma((supers,)), dma((supers,)),
    ]
    return pl.pallas_call(
        functools.partial(kernel, n_rows, n_cols, x_his),
        out_shape=(
            jax.ShapeDtypeStruct((supers, BS, width), F32),
            jax.ShapeDtypeStruct((supers, width, width), F32),
        ),
        in_specs=[pl.BlockSpec(memory_space=pl.ANY), vmem, smem, smem, smem, smem],
        out_specs=(vmem, vmem),
        scratch_shapes=scratch,
        compiler_params=pltpu.CompilerParams(
            collective_id=0, has_side_effects=True, vmem_limit_bytes=60 * 2**20
        ),
    )(blocks, panels, *lists)


def solution(mesh):
    n_rows, n_cols = mesh.shape["row"], mesh.shape["col"]
    return jax.shard_map(
        functools.partial(local, n_rows, n_cols),
        mesh=mesh,
        in_specs=(P("row", "col"), P(None, "col", None), P(), P()),
        out_specs=(P(None, ("row", "col"), None), P()),
        check_vma=False,
    )
```

```python
import functools

import jax
import jax.numpy as jnp
from jax import lax
from jax.experimental import pallas as pl
from jax.experimental.pallas import tpu as pltpu
from jax.sharding import PartitionSpec as P

BS = 128
MESH = pl.DeviceIdType.MESH
F32 = jnp.float32
BF16 = jnp.bfloat16


def tables(block_slot, list_ids, n_rows, n_cols):
    n_blocks, listed = block_slot.shape[0], list_ids.shape[1]
    ids = jnp.arange(n_blocks, dtype=jnp.int32)
    slots = jnp.sum(jnp.where(list_ids[..., None] == ids, block_slot, 0), axis=-1)
    col_blocks, row_blocks = n_blocks // n_cols, n_blocks // n_rows
    row = slots // row_blocks
    pos = jnp.arange(listed, dtype=jnp.int32)
    before = pos[None, :] < pos[:, None]
    kth = jnp.sum(((row[:, :, None] == row[:, None, :]) & before).astype(jnp.int32), axis=-1)
    key = row * n_cols + kth
    keys = jnp.arange(n_rows * n_cols, dtype=jnp.int32)
    code = jnp.sum(jnp.where(key[:, None, :] == keys[:, None], (1 + slots * listed + pos)[:, None, :], 0), axis=-1)
    slot, place = jnp.maximum(code - 1, 0) // listed, jnp.maximum(code - 1, 0) % listed
    shard = listed // n_cols
    table = jnp.stack(
        [
            (code > 0).astype(jnp.int32), place // shard, slot // col_blocks, slot % col_blocks, slot % row_blocks,
            slot // col_blocks % 2,
        ]
    )
    return slots // col_blocks, table


def kernel(
    n_rows, n_cols, x_his,
    inv_hbm, pan, cols, by_k,
    out, diag,
    a_all, a_pick, p_send, p_recv, p_all, l_recv, left,
    part, core_recv, z_recv, x_recv, d_part, d_sib, d_row, d_row_in, d_col, d_col_in, e_piece, e_col, e_row,
    a_sem, p_ss, p_rs, b_ss, b_rs, ag_ss, ag_rs, as_ss, as_rs, l_ss, l_rs, m_ss, m_rs, c_ss, c_rs, z_ss, z_rs, x_ss, x_rs,
    ds_ss, ds_rs, dr_ss, dr_rs, dc_ss, dc_rs, ec_ss, ec_rs, er_ss, er_rs, es_ss, es_rs,
):
    supers = pan.shape[0]
    sub = BS // n_rows
    col_blocks = a_all.shape[0]
    shard = pan.shape[1] // BS
    width = pan.shape[2]
    chips = n_cols // 2
    zs = chips // x_his
    ys = n_rows // 2
    me_r, me_c = lax.axis_index("row"), lax.axis_index("col")
    core = lax.rem(me_c, 2)
    chip = me_c // 2
    x_hi, z = chip // zs, lax.rem(chip, zs)
    sibling = (me_r, me_c + 1 - 2 * core)

    def remote(src, dst, ss, rs, to):
        return pltpu.make_async_remote_copy(
            src_ref=src, dst_ref=dst, send_sem=ss, recv_sem=rs, device_id=to, device_id_type=MESH
        )

    def load_a(b):
        columns = pl.ds(pl.multiple_of(b * BS, BS), BS)
        return pltpu.make_async_copy(inv_hbm.at[:, :, columns], a_all.at[b], a_sem.at[b])

    @pl.loop(0, col_blocks)
    def _(b):
        load_a(b).start()

    barrier = pltpu.get_barrier_semaphore()

    @pl.loop(1, n_cols)
    def _(d):
        pl.semaphore_signal(barrier, inc=1, device_id=(me_r, lax.rem(me_c + d, n_cols)), device_id_type=MESH)

    @pl.loop(1, n_rows)
    def _(d):
        pl.semaphore_signal(barrier, inc=1, device_id=(lax.rem(me_r + d, n_rows), me_c), device_id_type=MESH)

    def pick_for(c, s):
        piece = jnp.zeros((sub, width), BF16)
        for q in range(shard):
            block = pan[s, pl.ds(pl.multiple_of(q * BS + me_r * sub, sub), sub), :]
            piece = jnp.where(cols[s, me_c * shard + q] == c, block, piece)
        return piece

    @pl.loop(1, n_cols)
    def _(d):
        for s in range(supers):
            p_send[d, s] = pick_for(lax.rem(me_c + d, n_cols), s)

    for s in range(supers):
        p_recv[core, me_c, s] = pick_for(me_c, s)

    pl.semaphore_wait(barrier, n_cols + n_rows - 2)

    def p_copy(d, source):
        to = (me_r, lax.rem(me_c + d, n_cols))
        return remote(p_send.at[d], p_recv.at[lax.rem(to[1], 2), source], p_ss.at[d], p_rs.at[d], to)

    @pl.loop(1, n_cols)
    def _(d):
        p_copy(d, me_c).start()

    def picks(s):
        @pl.loop(0, n_cols)
        def _(i):
            half_of, place = i // chips, lax.rem(i, chips)
            k = 2 * place + jnp.where(half_of == 1, core, 1 - core)
            a_row = by_k[4, s, me_r * n_cols + k]
            rows = pl.ds(pl.multiple_of(i * BS, BS), BS)
            for b in range(n_cols):
                block = a_all[by_k[3, s, chip * n_cols + b], a_row]
                here = by_k[0, s, chip * n_cols + b] * (by_k[2, s, chip * n_cols + b] == me_c) == 1
                a_pick[s, rows, b * BS : (b + 1) * BS] = jnp.where(here, block, jnp.zeros_like(block))

    @pl.loop(0, col_blocks)
    def _(b):
        load_a(b).wait()

    picks(0)

    @pl.loop(1, n_cols)
    def _(d):
        source = lax.rem(me_c - d + n_cols, n_cols)
        remote(p_send.at[d], p_recv.at[core, source], p_ss.at[d], p_rs.at[d], sibling).wait_recv()

    def b_copy(of):
        return remote(p_recv.at[of], p_recv.at[of], b_ss, b_rs, sibling)

    b_copy(core).start()
    b_copy(1 - core).wait_recv()

    mine = pl.ds(core * chips, chips)
    x_lo, y = me_r // ys, lax.rem(me_r, ys)
    up, down, across = x_lo * ys + lax.rem(y + 1, ys), x_lo * ys + lax.rem(y + ys - 1, ys), (1 - x_lo) * ys + y
    far = x_lo * ys + lax.rem(y + 2, ys)
    far_up, far_down = lax.rem(up + ys, n_rows), lax.rem(down + ys, n_rows)
    far_far = lax.rem(far + ys, n_rows)
    first = pl.ds(core * chips, chips // 2)
    second = pl.ds(core * chips + chips // 2, chips // 2)

    def ag_copy(s, j, slots, source, to):
        block = p_all.at[s, slots, source]
        return remote(block, block, ag_ss.at[s, j], ag_rs.at[s, j], (to, me_c))

    sends = {
        0: (mine, me_r, up), 1: (mine, me_r, down), 2: (mine, me_r, across),
        3: (first, down, up), 4: (second, up, down), 5: (mine, across, up), 6: (mine, across, down), 7: (mine, far, across),
    }
    arrivals = {
        0: (mine, down), 1: (mine, up), 2: (mine, across),
        3: (first, far), 4: (second, far), 5: (mine, far_down), 6: (mine, far_up), 7: (mine, far_far),
    }

    def ag_start(s, j):
        ag_copy(s, j, *sends[j]).start()

    def ag_wait(s, j):
        ag_copy(s, j, *arrivals[j], across).wait_recv()

    def as_copy(s, source, of):
        block = p_all.at[s, pl.ds(of * chips, chips), source]
        return remote(block, block, as_ss.at[s, source], as_rs.at[s, source], sibling)

    def pack(s):
        for t in range(chips):
            k = core * chips + t
            block = p_recv[by_k[5, s, chip * n_cols + k], by_k[1, s, chip * n_cols + k], s]
            valid = by_k[0, s, chip * n_cols + k] == 1
            p_all[s, k, me_r] = jnp.where(valid, block, jnp.zeros_like(block))

    def ag_first(s):
        for j in (0, 1, 2):
            ag_start(s, j)
        as_copy(s, me_r, core).start()

    def ag_second(s):
        ag_wait(s, 2)
        ag_start(s, 5)
        ag_start(s, 6)
        ag_wait(s, 0)
        ag_start(s, 3)
        ag_wait(s, 1)
        ag_start(s, 4)
        for source in (across, down, up):
            as_copy(s, source, core).start()

    def ag_third(s):
        ag_wait(s, 3)
        ag_wait(s, 4)
        ag_start(s, 7)
        ag_wait(s, 5)
        ag_wait(s, 6)
        for source in (far, far_down, far_up):
            as_copy(s, source, core).start()
        ag_wait(s, 7)
        as_copy(s, far_far, core).start()

    def l_copy(t):
        k = core * chips + t
        return remote(p_all.at[:, k, me_r], l_recv.at[chip], l_ss.at[t], l_rs.at[chip], (me_r, k))

    def l_arrive(j):
        return remote(p_all.at[:, 0, me_r], l_recv.at[j], l_ss.at[0], l_rs.at[j], sibling)

    def l_first():
        @pl.loop(0, chips)
        def _(t):
            k = core * chips + t

            @pl.when(k != me_c)
            def _():
                l_copy(t).start()

            @pl.when(k == me_c)
            def _():
                l_recv[chip] = p_all[:, k, me_r]

    def m_copy(d):
        g = lax.rem(me_r + d, n_rows)
        return remote(l_recv.at[g], left.at[:, me_r], m_ss.at[d], m_rs.at[d], (g, me_c))

    def m_arrive(d):
        source = lax.rem(me_r - d + n_rows, n_rows)
        return remote(l_recv.at[0], left.at[:, source], m_ss.at[d], m_rs.at[d], (source, me_c))

    def l_second():
        @pl.loop(0, chips)
        def _(j):
            @pl.when(2 * j + me_c // chips != me_c)
            def _():
                l_arrive(j).wait_recv()

        left[:, me_r] = l_recv[me_r]

        @pl.loop(1, n_rows)
        def _(d):
            m_copy(d).start()

    pack(0)
    ag_first(0)
    pack(1)
    picks(1)
    ag_second(0)
    ag_first(1)
    l_first()
    ag_third(0)
    ag_second(1)

    def c_copy(s, h):
        return remote(part.at[s, 0, h], core_recv.at[s, h], c_ss.at[s, h], c_rs.at[s, h], sibling)

    def z_copy(s, h, d):
        to = (me_r, (x_hi * zs + lax.rem(z + d, zs)) * 2 + core)
        return remote(part.at[s, 1, h, lax.rem(z + d, zs)], z_recv.at[s, h, d], z_ss.at[s, h, d], z_rs.at[s, h, d], to)

    def products(s):
        @pl.loop(0, n_rows)
        def _(source):
            as_copy(s, source, 1 - core).wait_recv()

        @pl.loop(0, 2 * x_his)
        def _(i):
            half_of, h = i // x_his, lax.rem(i + 1 + x_hi, x_his)
            rows = pl.ds(pl.multiple_of((half_of * chips + h * zs) * BS, BS), zs * BS)
            product = jnp.dot(a_pick[s, rows, :], p_all[s].reshape(n_cols * BS, width), preferred_element_type=F32)
            part[s, half_of, h] = product.reshape(zs, BS, width)

            @pl.when(half_of == 0)
            def _():
                c_copy(s, h).start()

        for h in (1 - x_hi, x_hi):
            c_copy(s, h).wait_recv()
            part[s, 1, h] = part[s, 1, h] + core_recv[s, h]
            for d in range(1, zs):
                z_copy(s, h, d).start()

    products(0)
    l_second()
    ag_third(1)
    products(1)

    @pl.loop(1, n_rows)
    def _(d):
        m_arrive(d).wait_recv()

    def x_copy(s):
        to = (me_r, ((1 - x_hi) * zs + z) * 2 + core)
        return remote(part.at[s, 1, 1 - x_hi, z], x_recv.at[s], x_ss.at[s], x_rs.at[s], to)

    def over_z(s, h):
        total = part[s, 1, h, z]
        for d in range(1, zs):
            z_copy(s, h, d).wait_recv()
            total = total + z_recv[s, h, d]
        part[s, 1, h, z] = total

    half = width // 2
    piece = half // n_rows

    def ds_copy(s):
        there = pl.ds(pl.multiple_of((1 - core) * half, half), half)
        return remote(d_part.at[s, there], d_sib.at[s], ds_ss.at[s], ds_rs.at[s], sibling)

    def dr_copy(s, d):
        g = lax.rem(me_r + d, n_rows)
        return remote(d_row.at[s, g], d_row_in.at[s, d], dr_ss.at[s, d], dr_rs.at[s, d], (g, me_c))

    def chip_at(d):
        return lax.rem(chip + d, chips)

    def dc_copy(s, d):
        t = chip_at(d)
        return remote(d_col.at[s, t], d_col_in.at[s, d], dc_ss.at[s, d], dc_rs.at[s, d], (me_r, 2 * t + core))

    def ec_copy(s, d, source):
        return remote(e_piece.at[s], e_col.at[s, source], ec_ss.at[s, d], ec_rs.at[s, d], (me_r, 2 * chip_at(d) + core))

    def rows_of(r):
        return pl.ds(pl.multiple_of(core * half + r * piece, piece), piece)

    def er_copy(s, d, source):
        to = (lax.rem(me_r + d, n_rows), me_c)
        return remote(e_row.at[s], diag.at[s, rows_of(source)], er_ss.at[s, d], er_rs.at[s, d], to)

    def es_copy(s, half_of):
        there = pl.ds(pl.multiple_of(half_of * half, half), half)
        return remote(diag.at[s, there], diag.at[s, there], es_ss.at[s], es_rs.at[s], sibling)

    def finish_sums(s):
        x_copy(s).wait_recv()
        total = part[s, 1, x_hi, z] + x_recv[s]
        valid = by_k[0, s, me_r * n_cols + me_c] == 1
        total = jnp.where(valid, total, jnp.zeros_like(total))
        out[s] = total
        high = total.astype(BF16)
        low = (total - high.astype(F32)).astype(BF16)
        block = left[s].reshape(BS, width)
        contract = functools.partial(
            lax.dot_general, dimension_numbers=(((0,), (0,)), ((), ())), preferred_element_type=F32
        )
        d_part[s] = -(contract(block, high) + contract(block, low))
        ds_copy(s).start()

    def over_cores(s):
        ds_copy(s).wait_recv()
        here = pl.ds(pl.multiple_of(core * half, half), half)
        total = d_part[s, here] + d_sib[s]
        d_row[s] = total.reshape(n_rows, piece, width)

        @pl.loop(1, n_rows)
        def _(d):
            dr_copy(s, d).start()

    def over_rows(s):
        total = d_row[s, me_r]
        for d in range(1, n_rows):
            dr_copy(s, d).wait_recv()
            total = total + d_row_in[s, d]
        for t in range(chips):
            d_col[s, t] = total[(t // 2) * 8 : (t // 2) * 8 + 8, (t % 2) * half : (t % 2) * half + half]

        @pl.loop(1, chips)
        def _(d):
            dc_copy(s, d).start()

    def over_chips(s):
        total = d_col[s, chip]
        for d in range(1, chips):
            dc_copy(s, d).wait_recv()
            total = total + d_col_in[s, d]
        e_piece[s] = total
        e_col[s, chip] = total

        @pl.loop(1, chips)
        def _(d):
            ec_copy(s, d, chip).start()

    def back_over_chips(s):
        @pl.loop(1, chips)
        def _(d):
            ec_copy(s, d, lax.rem(chip - d + chips, chips)).wait_recv()

        for t in range(chips):
            e_row[s, (t // 2) * 8 : (t // 2) * 8 + 8, (t % 2) * half : (t % 2) * half + half] = e_col[s, t]
        diag[s, rows_of(me_r)] = e_row[s]

        @pl.loop(1, n_rows)
        def _(d):
            er_copy(s, d, me_r).start()

    def back_over_rows(s):
        @pl.loop(1, n_rows)
        def _(d):
            er_copy(s, d, lax.rem(me_r - d + n_rows, n_rows)).wait_recv()

        es_copy(s, core).start()

    over_z(0, 1 - x_hi)
    x_copy(0).start()
    over_z(0, x_hi)
    finish_sums(0)
    over_cores(0)
    over_z(1, 1 - x_hi)
    x_copy(1).start()
    over_z(1, x_hi)
    over_rows(0)
    finish_sums(1)
    over_cores(1)
    over_chips(0)
    over_rows(1)
    back_over_chips(0)
    over_chips(1)
    back_over_rows(0)
    back_over_chips(1)
    back_over_rows(1)

    @pl.loop(1, n_cols)
    def _(d):
        p_copy(d, me_c).wait_send()

    b_copy(core).wait_send()

    @pl.loop(0, chips)
    def _(t):
        @pl.when(core * chips + t != me_c)
        def _():
            l_copy(t).wait_send()

    @pl.loop(1, n_rows)
    def _(d):
        m_copy(d).wait_send()

    for s in range(supers):
        for j in sends:
            ag_copy(s, j, *sends[j]).wait_send()

        @pl.loop(0, n_rows)
        def _(source, s=s):
            as_copy(s, source, core).wait_send()

        @pl.loop(1, n_rows)
        def _(d, s=s):
            dr_copy(s, d).wait_send()
            er_copy(s, d, me_r).wait_send()

        @pl.loop(1, chips)
        def _(d, s=s):
            dc_copy(s, d).wait_send()
            ec_copy(s, d, chip).wait_send()

        for h in range(x_his):
            c_copy(s, h).wait_send()
            for d in range(1, zs):
                z_copy(s, h, d).wait_send()
        x_copy(s).wait_send()
        ds_copy(s).wait_send()
        es_copy(s, core).wait_send()
        es_copy(s, 1 - core).wait_recv()


def local(n_rows, n_cols, inverse, panels, block_slot, list_ids):
    supers, _, width = panels.shape
    col_blocks = inverse.shape[1] // BS
    sub = BS // n_rows
    x_his = 2
    chips = n_cols // 2
    zs = chips // x_his
    half = width // 2
    piece = half // n_rows
    lists = tables(block_slot, list_ids, n_rows, n_cols)
    blocks = inverse.reshape(-1, BS, inverse.shape[1])
    vmem = pl.BlockSpec(memory_space=pltpu.VMEM)
    smem = pl.BlockSpec(memory_space=pltpu.SMEM)
    dma = pltpu.SemaphoreType.DMA
    scratch = [
        pltpu.VMEM((col_blocks, blocks.shape[0], BS, BS), BF16),
        pltpu.VMEM((supers, n_cols * BS, n_cols * BS), BF16),
        pltpu.VMEM((n_cols, supers, sub, width), BF16),
        pltpu.VMEM((2, n_cols, supers, sub, width), BF16),
        pltpu.VMEM((supers, n_cols, n_rows, sub, width), BF16),
        pltpu.VMEM((chips, supers, sub, width), BF16),
        pltpu.VMEM((supers, n_rows, sub, width), BF16),
        pltpu.VMEM((supers, 2, x_his, zs, BS, width), F32),
        pltpu.VMEM((supers, x_his, zs, BS, width), F32),
        pltpu.VMEM((supers, x_his, zs, BS, width), F32),
        pltpu.VMEM((supers, BS, width), F32),
        pltpu.VMEM((supers, width, width), F32),
        pltpu.VMEM((supers, half, width), F32),
        pltpu.VMEM((supers, n_rows, piece, width), F32),
        pltpu.VMEM((supers, n_rows, piece, width), F32),
        pltpu.VMEM((supers, chips, 8, half), F32),
        pltpu.VMEM((supers, chips, 8, half), F32),
        pltpu.VMEM((supers, 8, half), F32),
        pltpu.VMEM((supers, chips, 8, half), F32),
        pltpu.VMEM((supers, piece, width), F32),
        dma((col_blocks,)),
        dma((n_cols,)), dma((n_cols,)),
        dma(()), dma(()),
        dma((supers, 8)), dma((supers, 8)),
        dma((supers, n_rows)), dma((supers, n_rows)),
        dma((chips,)), dma((chips,)),
        dma((n_rows,)), dma((n_rows,)),
        dma((supers, x_his)), dma((supers, x_his)),
        dma((supers, x_his, zs)), dma((supers, x_his, zs)),
        dma((supers,)), dma((supers,)),
        dma((supers,)), dma((supers,)),
        dma((supers, n_rows)), dma((supers, n_rows)),
        dma((supers, chips)), dma((supers, chips)),
        dma((supers, chips)), dma((supers, chips)),
        dma((supers, n_rows)), dma((supers, n_rows)),
        dma((supers,)), dma((supers,)),
    ]
    return pl.pallas_call(
        functools.partial(kernel, n_rows, n_cols, x_his),
        out_shape=(
            jax.ShapeDtypeStruct((supers, BS, width), F32),
            jax.ShapeDtypeStruct((supers, width, width), F32),
        ),
        in_specs=[pl.BlockSpec(memory_space=pl.ANY), vmem, smem, smem],
        out_specs=(vmem, vmem),
        scratch_shapes=scratch,
        compiler_params=pltpu.CompilerParams(
            collective_id=0, has_side_effects=True, vmem_limit_bytes=60 * 2**20
        ),
    )(blocks, panels, *lists)


def solution(mesh):
    n_rows, n_cols = mesh.shape["row"], mesh.shape["col"]
    return jax.shard_map(
        functools.partial(local, n_rows, n_cols),
        mesh=mesh,
        in_specs=(P("row", "col"), P(None, "col", None), P(), P()),
        out_specs=(P(None, ("row", "col"), None), P()),
        check_vma=False,
    )
```

```python
import functools

import jax
import jax.numpy as jnp
from jax import lax
from jax.experimental import pallas as pl
from jax.experimental.pallas import tpu as pltpu
from jax.sharding import PartitionSpec as P

BS = 128
MESH = pl.DeviceIdType.MESH
F32 = jnp.float32
BF16 = jnp.bfloat16


def tables(block_slot, list_ids, n_rows, n_cols):
    n_blocks, listed = block_slot.shape[0], list_ids.shape[1]
    ids = jnp.arange(n_blocks, dtype=jnp.int32)
    slots = jnp.sum(jnp.where(list_ids[..., None] == ids, block_slot, 0), axis=-1)
    col_blocks, row_blocks = n_blocks // n_cols, n_blocks // n_rows
    row = slots // row_blocks
    pos = jnp.arange(listed, dtype=jnp.int32)
    before = pos[None, :] < pos[:, None]
    kth = jnp.sum(((row[:, :, None] == row[:, None, :]) & before).astype(jnp.int32), axis=-1)
    key = row * n_cols + kth
    keys = jnp.arange(n_rows * n_cols, dtype=jnp.int32)
    code = jnp.sum(jnp.where(key[:, None, :] == keys[:, None], (1 + slots * listed + pos)[:, None, :], 0), axis=-1)
    slot, place = jnp.maximum(code - 1, 0) // listed, jnp.maximum(code - 1, 0) % listed
    shard = listed // n_cols
    table = jnp.stack(
        [
            (code > 0).astype(jnp.int32), place // shard, slot // col_blocks, slot % col_blocks, slot % row_blocks,
            slot // col_blocks % 2,
        ]
    )
    return slots // col_blocks, table


SCALE_ROWS = 16
TOP = 32000.0


def encode(ref, block):
    top = jnp.max(jnp.abs(block), axis=0, keepdims=True)
    exponent = jnp.floor(jnp.log2(jnp.maximum(top, 1e-30))) + 1.0
    coded = jnp.round(block * (jnp.exp2(-exponent) * TOP))
    ref[0:BS] = coded.astype(jnp.int32).astype(jnp.int16)
    exponents = jnp.broadcast_to(exponent, (SCALE_ROWS, block.shape[1]))
    ref[BS : BS + SCALE_ROWS] = exponents.astype(jnp.int32).astype(jnp.int16)


def decode(ref):
    exponent = ref[BS : BS + SCALE_ROWS].astype(jnp.int32).astype(F32)[0:1]
    return ref[0:BS].astype(jnp.int32).astype(F32) * (jnp.exp2(exponent) * (1.0 / TOP))


def kernel(
    n_rows, n_cols, x_his,
    inv_hbm, pan, cols, by_k,
    out, diag,
    a_all, a_pick, p_send, p_recv, p_all, l_recv, left,
    part, core_recv, z_send, z_recv, x_send, x_recv, d_part, d_sib, d_row, d_row_in, d_col, d_col_in, e_piece, e_col, e_row,
    a_sem, p_ss, p_rs, b_ss, b_rs, ag_ss, ag_rs, as_ss, as_rs, l_ss, l_rs, m_ss, m_rs, c_ss, c_rs, z_ss, z_rs, x_ss, x_rs,
    ds_ss, ds_rs, dr_ss, dr_rs, dc_ss, dc_rs, ec_ss, ec_rs, er_ss, er_rs, es_ss, es_rs,
):
    supers = pan.shape[0]
    sub = BS // n_rows
    col_blocks = a_all.shape[0]
    shard = pan.shape[1] // BS
    width = pan.shape[2]
    chips = n_cols // 2
    zs = chips // x_his
    ys = n_rows // 2
    me_r, me_c = lax.axis_index("row"), lax.axis_index("col")
    core = lax.rem(me_c, 2)
    chip = me_c // 2
    x_hi, z = chip // zs, lax.rem(chip, zs)
    sibling = (me_r, me_c + 1 - 2 * core)

    def remote(src, dst, ss, rs, to):
        return pltpu.make_async_remote_copy(
            src_ref=src, dst_ref=dst, send_sem=ss, recv_sem=rs, device_id=to, device_id_type=MESH
        )

    def load_a(b):
        columns = pl.ds(pl.multiple_of(b * BS, BS), BS)
        return pltpu.make_async_copy(inv_hbm.at[:, :, columns], a_all.at[b], a_sem.at[b])

    @pl.loop(0, col_blocks)
    def _(b):
        load_a(b).start()

    barrier = pltpu.get_barrier_semaphore()

    @pl.loop(1, n_cols)
    def _(d):
        pl.semaphore_signal(barrier, inc=1, device_id=(me_r, lax.rem(me_c + d, n_cols)), device_id_type=MESH)

    @pl.loop(1, n_rows)
    def _(d):
        pl.semaphore_signal(barrier, inc=1, device_id=(lax.rem(me_r + d, n_rows), me_c), device_id_type=MESH)

    def pick_for(c, s):
        piece = jnp.zeros((sub, width), BF16)
        for q in range(shard):
            block = pan[s, pl.ds(pl.multiple_of(q * BS + me_r * sub, sub), sub), :]
            piece = jnp.where(cols[s, me_c * shard + q] == c, block, piece)
        return piece

    @pl.loop(1, n_cols)
    def _(d):
        for s in range(supers):
            p_send[d, s] = pick_for(lax.rem(me_c + d, n_cols), s)

    for s in range(supers):
        p_recv[core, me_c, s] = pick_for(me_c, s)

    pl.semaphore_wait(barrier, n_cols + n_rows - 2)

    def p_copy(d, source):
        to = (me_r, lax.rem(me_c + d, n_cols))
        return remote(p_send.at[d], p_recv.at[lax.rem(to[1], 2), source], p_ss.at[d], p_rs.at[d], to)

    @pl.loop(1, n_cols)
    def _(d):
        p_copy(d, me_c).start()

    def picks(s):
        @pl.loop(0, n_cols)
        def _(i):
            half_of, place = i // chips, lax.rem(i, chips)
            k = 2 * place + jnp.where(half_of == 1, core, 1 - core)
            a_row = by_k[4, s, me_r * n_cols + k]
            rows = pl.ds(pl.multiple_of(i * BS, BS), BS)
            for b in range(n_cols):
                block = a_all[by_k[3, s, chip * n_cols + b], a_row]
                here = by_k[0, s, chip * n_cols + b] * (by_k[2, s, chip * n_cols + b] == me_c) == 1
                a_pick[s, rows, b * BS : (b + 1) * BS] = jnp.where(here, block, jnp.zeros_like(block))

    @pl.loop(0, col_blocks)
    def _(b):
        load_a(b).wait()

    picks(0)

    @pl.loop(1, n_cols)
    def _(d):
        source = lax.rem(me_c - d + n_cols, n_cols)
        remote(p_send.at[d], p_recv.at[core, source], p_ss.at[d], p_rs.at[d], sibling).wait_recv()

    def b_copy(of):
        return remote(p_recv.at[of], p_recv.at[of], b_ss, b_rs, sibling)

    b_copy(core).start()
    b_copy(1 - core).wait_recv()

    mine = pl.ds(core * chips, chips)
    x_lo, y = me_r // ys, lax.rem(me_r, ys)
    up, down, across = x_lo * ys + lax.rem(y + 1, ys), x_lo * ys + lax.rem(y + ys - 1, ys), (1 - x_lo) * ys + y
    far = x_lo * ys + lax.rem(y + 2, ys)
    far_up, far_down = lax.rem(up + ys, n_rows), lax.rem(down + ys, n_rows)
    far_far = lax.rem(far + ys, n_rows)
    first = pl.ds(core * chips, chips // 2)
    second = pl.ds(core * chips + chips // 2, chips // 2)

    def ag_copy(s, j, slots, source, to):
        block = p_all.at[s, slots, source]
        return remote(block, block, ag_ss.at[s, j], ag_rs.at[s, j], (to, me_c))

    sends = {
        0: (mine, me_r, up), 1: (mine, me_r, down), 2: (mine, me_r, across),
        3: (first, down, up), 4: (second, up, down), 5: (mine, across, up), 6: (mine, across, down), 7: (mine, far, across),
    }
    arrivals = {
        0: (mine, down), 1: (mine, up), 2: (mine, across),
        3: (first, far), 4: (second, far), 5: (mine, far_down), 6: (mine, far_up), 7: (mine, far_far),
    }

    def ag_start(s, j):
        ag_copy(s, j, *sends[j]).start()

    def ag_wait(s, j):
        ag_copy(s, j, *arrivals[j], across).wait_recv()

    def as_copy(s, source, of):
        block = p_all.at[s, pl.ds(of * chips, chips), source]
        return remote(block, block, as_ss.at[s, source], as_rs.at[s, source], sibling)

    def pack(s):
        for t in range(chips):
            k = core * chips + t
            block = p_recv[by_k[5, s, chip * n_cols + k], by_k[1, s, chip * n_cols + k], s]
            valid = by_k[0, s, chip * n_cols + k] == 1
            p_all[s, k, me_r] = jnp.where(valid, block, jnp.zeros_like(block))

    def ag_first(s):
        for j in (0, 1, 2):
            ag_start(s, j)
        as_copy(s, me_r, core).start()

    def ag_second(s):
        ag_wait(s, 2)
        ag_start(s, 5)
        ag_start(s, 6)
        ag_wait(s, 0)
        ag_start(s, 3)
        ag_wait(s, 1)
        ag_start(s, 4)
        for source in (across, down, up):
            as_copy(s, source, core).start()

    def ag_third(s):
        ag_wait(s, 3)
        ag_wait(s, 4)
        ag_start(s, 7)
        ag_wait(s, 5)
        ag_wait(s, 6)
        for source in (far, far_down, far_up):
            as_copy(s, source, core).start()
        ag_wait(s, 7)
        as_copy(s, far_far, core).start()

    def l_copy(t):
        k = core * chips + t
        return remote(p_all.at[:, k, me_r], l_recv.at[chip], l_ss.at[t], l_rs.at[chip], (me_r, k))

    def l_arrive(j):
        return remote(p_all.at[:, 0, me_r], l_recv.at[j], l_ss.at[0], l_rs.at[j], sibling)

    def l_first():
        @pl.loop(0, chips)
        def _(t):
            k = core * chips + t

            @pl.when(k != me_c)
            def _():
                l_copy(t).start()

            @pl.when(k == me_c)
            def _():
                l_recv[chip] = p_all[:, k, me_r]

    def m_copy(d):
        g = lax.rem(me_r + d, n_rows)
        return remote(l_recv.at[g], left.at[:, me_r], m_ss.at[d], m_rs.at[d], (g, me_c))

    def m_arrive(d):
        source = lax.rem(me_r - d + n_rows, n_rows)
        return remote(l_recv.at[0], left.at[:, source], m_ss.at[d], m_rs.at[d], (source, me_c))

    def l_second():
        @pl.loop(0, chips)
        def _(j):
            @pl.when(2 * j + me_c // chips != me_c)
            def _():
                l_arrive(j).wait_recv()

        left[:, me_r] = l_recv[me_r]

        @pl.loop(1, n_rows)
        def _(d):
            m_copy(d).start()

    pack(0)
    ag_first(0)
    pack(1)
    picks(1)
    ag_second(0)
    ag_first(1)
    l_first()
    ag_third(0)
    ag_second(1)

    def c_copy(s, h):
        return remote(part.at[s, 0, h], core_recv.at[s, h], c_ss.at[s, h], c_rs.at[s, h], sibling)

    def z_copy(s, h, d):
        to = (me_r, (x_hi * zs + lax.rem(z + d, zs)) * 2 + core)
        return remote(z_send.at[s, h, d], z_recv.at[s, h, d], z_ss.at[s, h, d], z_rs.at[s, h, d], to)

    def products(s):
        @pl.loop(0, n_rows)
        def _(source):
            as_copy(s, source, 1 - core).wait_recv()

        @pl.loop(0, 2 * x_his)
        def _(i):
            half_of, h = i // x_his, lax.rem(i + 1 + x_hi, x_his)
            rows = pl.ds(pl.multiple_of((half_of * chips + h * zs) * BS, BS), zs * BS)
            product = jnp.dot(a_pick[s, rows, :], p_all[s].reshape(n_cols * BS, width), preferred_element_type=F32)
            part[s, half_of, h] = product.reshape(zs, BS, width)

            @pl.when(half_of == 0)
            def _():
                c_copy(s, h).start()

        for h in (1 - x_hi, x_hi):
            c_copy(s, h).wait_recv()

            @pl.loop(1, zs)
            def _(d, h=h):
                there = lax.rem(z + d, zs)
                encode(z_send.at[s, h, d], part[s, 1, h, there] + core_recv[s, h, there])
                z_copy(s, h, d).start()

    products(0)
    l_second()
    ag_third(1)
    products(1)

    @pl.loop(1, n_rows)
    def _(d):
        m_arrive(d).wait_recv()

    def x_copy(s):
        to = (me_r, ((1 - x_hi) * zs + z) * 2 + core)
        return remote(x_send.at[s], x_recv.at[s], x_ss.at[s], x_rs.at[s], to)

    def over_z(s, h):
        total = part[s, 1, h, z] + core_recv[s, h, z]
        for d in range(1, zs):
            z_copy(s, h, d).wait_recv()
            total = total + decode(z_recv.at[s, h, d])
        return total

    def start_x(s):
        encode(x_send.at[s], over_z(s, 1 - x_hi))
        x_copy(s).start()

    half = width // 2
    piece = half // n_rows

    def ds_copy(s):
        there = pl.ds(pl.multiple_of((1 - core) * half, half), half)
        return remote(d_part.at[s, there], d_sib.at[s], ds_ss.at[s], ds_rs.at[s], sibling)

    def dr_copy(s, d):
        g = lax.rem(me_r + d, n_rows)
        return remote(d_row.at[s, g], d_row_in.at[s, d], dr_ss.at[s, d], dr_rs.at[s, d], (g, me_c))

    def chip_at(d):
        return lax.rem(chip + d, chips)

    def dc_copy(s, d):
        t = chip_at(d)
        return remote(d_col.at[s, t], d_col_in.at[s, d], dc_ss.at[s, d], dc_rs.at[s, d], (me_r, 2 * t + core))

    def ec_copy(s, d, source):
        return remote(e_piece.at[s], e_col.at[s, source], ec_ss.at[s, d], ec_rs.at[s, d], (me_r, 2 * chip_at(d) + core))

    def rows_of(r):
        return pl.ds(pl.multiple_of(core * half + r * piece, piece), piece)

    def er_copy(s, d, source):
        to = (lax.rem(me_r + d, n_rows), me_c)
        return remote(e_row.at[s], diag.at[s, rows_of(source)], er_ss.at[s, d], er_rs.at[s, d], to)

    def es_copy(s, half_of):
        there = pl.ds(pl.multiple_of(half_of * half, half), half)
        return remote(diag.at[s, there], diag.at[s, there], es_ss.at[s], es_rs.at[s], sibling)

    def finish_sums(s):
        total = over_z(s, x_hi)
        x_copy(s).wait_recv()
        total = total + decode(x_recv.at[s])
        valid = by_k[0, s, me_r * n_cols + me_c] == 1
        total = jnp.where(valid, total, jnp.zeros_like(total))
        out[s] = total
        high = total.astype(BF16)
        low = (total - high.astype(F32)).astype(BF16)
        block = left[s].reshape(BS, width)
        contract = functools.partial(
            lax.dot_general, dimension_numbers=(((0,), (0,)), ((), ())), preferred_element_type=F32
        )
        d_part[s] = -(contract(block, high) + contract(block, low))
        ds_copy(s).start()

    def over_cores(s):
        ds_copy(s).wait_recv()
        here = pl.ds(pl.multiple_of(core * half, half), half)
        total = d_part[s, here] + d_sib[s]
        d_row[s] = total.reshape(n_rows, piece, width)

        @pl.loop(1, n_rows)
        def _(d):
            dr_copy(s, d).start()

    def over_rows(s):
        total = d_row[s, me_r]
        for d in range(1, n_rows):
            dr_copy(s, d).wait_recv()
            total = total + d_row_in[s, d]
        for t in range(chips):
            d_col[s, t] = total[(t // 2) * 8 : (t // 2) * 8 + 8, (t % 2) * half : (t % 2) * half + half]

        @pl.loop(1, chips)
        def _(d):
            dc_copy(s, d).start()

    def over_chips(s):
        total = d_col[s, chip]
        for d in range(1, chips):
            dc_copy(s, d).wait_recv()
            total = total + d_col_in[s, d]
        e_piece[s] = total
        e_col[s, chip] = total

        @pl.loop(1, chips)
        def _(d):
            ec_copy(s, d, chip).start()

    def back_over_chips(s):
        @pl.loop(1, chips)
        def _(d):
            ec_copy(s, d, lax.rem(chip - d + chips, chips)).wait_recv()

        for t in range(chips):
            e_row[s, (t // 2) * 8 : (t // 2) * 8 + 8, (t % 2) * half : (t % 2) * half + half] = e_col[s, t]
        diag[s, rows_of(me_r)] = e_row[s]

        @pl.loop(1, n_rows)
        def _(d):
            er_copy(s, d, me_r).start()

    def back_over_rows(s):
        @pl.loop(1, n_rows)
        def _(d):
            er_copy(s, d, lax.rem(me_r - d + n_rows, n_rows)).wait_recv()

        es_copy(s, core).start()

    start_x(0)
    finish_sums(0)
    over_cores(0)
    start_x(1)
    over_rows(0)
    finish_sums(1)
    over_cores(1)
    over_chips(0)
    over_rows(1)
    back_over_chips(0)
    over_chips(1)
    back_over_rows(0)
    back_over_chips(1)
    back_over_rows(1)

    @pl.loop(1, n_cols)
    def _(d):
        p_copy(d, me_c).wait_send()

    b_copy(core).wait_send()

    @pl.loop(0, chips)
    def _(t):
        @pl.when(core * chips + t != me_c)
        def _():
            l_copy(t).wait_send()

    @pl.loop(1, n_rows)
    def _(d):
        m_copy(d).wait_send()

    for s in range(supers):
        for j in sends:
            ag_copy(s, j, *sends[j]).wait_send()

        @pl.loop(0, n_rows)
        def _(source, s=s):
            as_copy(s, source, core).wait_send()

        @pl.loop(1, n_rows)
        def _(d, s=s):
            dr_copy(s, d).wait_send()
            er_copy(s, d, me_r).wait_send()

        @pl.loop(1, chips)
        def _(d, s=s):
            dc_copy(s, d).wait_send()
            ec_copy(s, d, chip).wait_send()

        for h in range(x_his):
            c_copy(s, h).wait_send()
            for d in range(1, zs):
                z_copy(s, h, d).wait_send()
        x_copy(s).wait_send()
        ds_copy(s).wait_send()
        es_copy(s, core).wait_send()
        es_copy(s, 1 - core).wait_recv()


def local(n_rows, n_cols, inverse, panels, block_slot, list_ids):
    supers, _, width = panels.shape
    col_blocks = inverse.shape[1] // BS
    sub = BS // n_rows
    x_his = 2
    chips = n_cols // 2
    zs = chips // x_his
    half = width // 2
    piece = half // n_rows
    lists = tables(block_slot, list_ids, n_rows, n_cols)
    blocks = inverse.reshape(-1, BS, inverse.shape[1])
    vmem = pl.BlockSpec(memory_space=pltpu.VMEM)
    smem = pl.BlockSpec(memory_space=pltpu.SMEM)
    dma = pltpu.SemaphoreType.DMA
    scratch = [
        pltpu.VMEM((col_blocks, blocks.shape[0], BS, BS), BF16),
        pltpu.VMEM((supers, n_cols * BS, n_cols * BS), BF16),
        pltpu.VMEM((n_cols, supers, sub, width), BF16),
        pltpu.VMEM((2, n_cols, supers, sub, width), BF16),
        pltpu.VMEM((supers, n_cols, n_rows, sub, width), BF16),
        pltpu.VMEM((chips, supers, sub, width), BF16),
        pltpu.VMEM((supers, n_rows, sub, width), BF16),
        pltpu.VMEM((supers, 2, x_his, zs, BS, width), F32),
        pltpu.VMEM((supers, x_his, zs, BS, width), F32),
        pltpu.VMEM((supers, x_his, zs, BS + SCALE_ROWS, width), jnp.int16),
        pltpu.VMEM((supers, x_his, zs, BS + SCALE_ROWS, width), jnp.int16),
        pltpu.VMEM((supers, BS + SCALE_ROWS, width), jnp.int16),
        pltpu.VMEM((supers, BS + SCALE_ROWS, width), jnp.int16),
        pltpu.VMEM((supers, width, width), F32),
        pltpu.VMEM((supers, half, width), F32),
        pltpu.VMEM((supers, n_rows, piece, width), F32),
        pltpu.VMEM((supers, n_rows, piece, width), F32),
        pltpu.VMEM((supers, chips, 8, half), F32),
        pltpu.VMEM((supers, chips, 8, half), F32),
        pltpu.VMEM((supers, 8, half), F32),
        pltpu.VMEM((supers, chips, 8, half), F32),
        pltpu.VMEM((supers, piece, width), F32),
        dma((col_blocks,)),
        dma((n_cols,)), dma((n_cols,)),
        dma(()), dma(()),
        dma((supers, 8)), dma((supers, 8)),
        dma((supers, n_rows)), dma((supers, n_rows)),
        dma((chips,)), dma((chips,)),
        dma((n_rows,)), dma((n_rows,)),
        dma((supers, x_his)), dma((supers, x_his)),
        dma((supers, x_his, zs)), dma((supers, x_his, zs)),
        dma((supers,)), dma((supers,)),
        dma((supers,)), dma((supers,)),
        dma((supers, n_rows)), dma((supers, n_rows)),
        dma((supers, chips)), dma((supers, chips)),
        dma((supers, chips)), dma((supers, chips)),
        dma((supers, n_rows)), dma((supers, n_rows)),
        dma((supers,)), dma((supers,)),
    ]
    return pl.pallas_call(
        functools.partial(kernel, n_rows, n_cols, x_his),
        out_shape=(
            jax.ShapeDtypeStruct((supers, BS, width), F32),
            jax.ShapeDtypeStruct((supers, width, width), F32),
        ),
        in_specs=[pl.BlockSpec(memory_space=pl.ANY), vmem, smem, smem],
        out_specs=(vmem, vmem),
        scratch_shapes=scratch,
        compiler_params=pltpu.CompilerParams(
            collective_id=0, has_side_effects=True, vmem_limit_bytes=60 * 2**20
        ),
    )(blocks, panels, *lists)


def solution(mesh):
    n_rows, n_cols = mesh.shape["row"], mesh.shape["col"]
    return jax.shard_map(
        functools.partial(local, n_rows, n_cols),
        mesh=mesh,
        in_specs=(P("row", "col"), P(None, "col", None), P(), P()),
        out_specs=(P(None, ("row", "col"), None), P()),
        check_vma=False,
    )
```

```python
import functools

import jax
import jax.numpy as jnp
from jax import lax
from jax.experimental import pallas as pl
from jax.experimental.pallas import tpu as pltpu
from jax.sharding import PartitionSpec as P

BS = 128
MESH = pl.DeviceIdType.MESH
F32 = jnp.float32
BF16 = jnp.bfloat16


def tables(block_slot, list_ids, n_rows, n_cols):
    n_blocks, listed = block_slot.shape[0], list_ids.shape[1]
    ids = jnp.arange(n_blocks, dtype=jnp.int32)
    slots = jnp.sum(jnp.where(list_ids[..., None] == ids, block_slot, 0), axis=-1)
    col_blocks, row_blocks = n_blocks // n_cols, n_blocks // n_rows
    row = slots // row_blocks
    pos = jnp.arange(listed, dtype=jnp.int32)
    before = pos[None, :] < pos[:, None]
    kth = jnp.sum(((row[:, :, None] == row[:, None, :]) & before).astype(jnp.int32), axis=-1)
    key = row * n_cols + kth
    keys = jnp.arange(n_rows * n_cols, dtype=jnp.int32)
    code = jnp.sum(jnp.where(key[:, None, :] == keys[:, None], (1 + slots * listed + pos)[:, None, :], 0), axis=-1)
    slot, place = jnp.maximum(code - 1, 0) // listed, jnp.maximum(code - 1, 0) % listed
    shard = listed // n_cols
    table = jnp.stack(
        [
            (code > 0).astype(jnp.int32), place // shard, slot // col_blocks, slot % col_blocks, slot % row_blocks,
            slot // col_blocks % 2,
        ]
    )
    return slots // col_blocks, table


SCALE_ROWS = 16
TOP = 32000.0


def encode(ref, block):
    top = jnp.max(jnp.abs(block), axis=0, keepdims=True)
    exponent = jnp.floor(jnp.log2(jnp.maximum(top, 1e-30))) + 1.0
    coded = jnp.round(block * (jnp.exp2(-exponent) * TOP))
    ref[0:BS] = coded.astype(jnp.int32).astype(jnp.int16)
    exponents = jnp.broadcast_to(exponent, (SCALE_ROWS, block.shape[1]))
    ref[BS : BS + SCALE_ROWS] = exponents.astype(jnp.int32).astype(jnp.int16)


def decode(ref):
    exponent = ref[BS : BS + SCALE_ROWS].astype(jnp.int32).astype(F32)[0:1]
    return ref[0:BS].astype(jnp.int32).astype(F32) * (jnp.exp2(exponent) * (1.0 / TOP))


def kernel(
    n_rows, n_cols, x_his,
    inv_hbm, pan, cols, by_k,
    out, diag,
    a_all, a_pick, p_send, p_recv_0, p_recv_1, p_all, l_recv, left,
    part, core_recv, z_send, z_recv, x_send, x_recv, d_part, d_sib, u_send, u_recv, v_send, v_recv, t_all,
    a_sem, p_ss, p_rs, b_ss, b_rs, ag_ss, ag_rs, as_ss, as_rs, l_ss, l_rs, m_ss, m_rs, c_ss, c_rs, z_ss, z_rs, x_ss, x_rs,
    ds_ss, ds_rs, u_ss, u_rs, v_ss, v_rs, t_ss, t_rs, w_ss, w_rs, er_ss, er_rs, es_ss, es_rs,
):
    supers = pan.shape[0]
    p_recv = (p_recv_0, p_recv_1)
    sub = BS // n_rows
    col_blocks = a_all.shape[0]
    shard = pan.shape[1] // BS
    width = pan.shape[2]
    chips = n_cols // 2
    zs = chips // x_his
    ys = n_rows // 2
    me_r, me_c = lax.axis_index("row"), lax.axis_index("col")
    core = lax.rem(me_c, 2)
    chip = me_c // 2
    x_hi, z = chip // zs, lax.rem(chip, zs)
    sibling = (me_r, me_c + 1 - 2 * core)

    def remote(src, dst, ss, rs, to):
        return pltpu.make_async_remote_copy(
            src_ref=src, dst_ref=dst, send_sem=ss, recv_sem=rs, device_id=to, device_id_type=MESH
        )

    def load_a(b):
        columns = pl.ds(pl.multiple_of(b * BS, BS), BS)
        return pltpu.make_async_copy(inv_hbm.at[:, :, columns], a_all.at[b], a_sem.at[b])

    @pl.loop(0, col_blocks)
    def _(b):
        load_a(b).start()

    barrier = pltpu.get_barrier_semaphore()

    @pl.loop(1, n_cols)
    def _(d):
        pl.semaphore_signal(barrier, inc=1, device_id=(me_r, lax.rem(me_c + d, n_cols)), device_id_type=MESH)

    @pl.loop(1, n_rows)
    def _(d):
        pl.semaphore_signal(barrier, inc=1, device_id=(lax.rem(me_r + d, n_rows), me_c), device_id_type=MESH)

    opposite = (lax.rem(me_r + ys, n_rows), lax.rem(me_c + zs * 2, n_cols))
    pl.semaphore_signal(barrier, inc=1, device_id=opposite, device_id_type=MESH)

    def pick_for(c, s):
        piece = jnp.zeros((sub, width), BF16)
        for q in range(shard):
            block = pan[s, pl.ds(pl.multiple_of(q * BS + me_r * sub, sub), sub), :]
            piece = jnp.where(cols[s, me_c * shard + q] == c, block, piece)
        return piece

    @pl.loop(1, n_cols)
    def _(d):
        for s in range(supers):
            p_send[s, d] = pick_for(lax.rem(me_c + d, n_cols), s)

    for s in range(supers):
        p_recv[s][core, me_c] = pick_for(me_c, s)

    pl.semaphore_wait(barrier, n_cols + n_rows - 1)

    def p_copy(s, d, source):
        to = (me_r, lax.rem(me_c + d, n_cols))
        return remote(p_send.at[s, d], p_recv[s].at[lax.rem(to[1], 2), source], p_ss.at[s, d], p_rs.at[s, d], to)

    for s in range(supers):
        @pl.loop(1, n_cols)
        def _(d, s=s):
            p_copy(s, d, me_c).start()

    def picks(s):
        @pl.loop(0, n_cols)
        def _(i):
            half_of, place = i // chips, lax.rem(i, chips)
            k = 2 * place + jnp.where(half_of == 1, core, 1 - core)
            a_row = by_k[4, s, me_r * n_cols + k]
            rows = pl.ds(pl.multiple_of(i * BS, BS), BS)
            for b in range(n_cols):
                block = a_all[by_k[3, s, chip * n_cols + b], a_row]
                here = by_k[0, s, chip * n_cols + b] * (by_k[2, s, chip * n_cols + b] == me_c) == 1
                a_pick[s, rows, b * BS : (b + 1) * BS] = jnp.where(here, block, jnp.zeros_like(block))

    @pl.loop(0, col_blocks)
    def _(b):
        load_a(b).wait()

    picks(0)

    def b_copy(s, of):
        return remote(p_recv[s].at[of], p_recv[s].at[of], b_ss.at[s], b_rs.at[s], sibling)

    def to_cores(s):
        @pl.loop(1, n_cols)
        def _(d):
            source = lax.rem(me_c - d + n_cols, n_cols)
            remote(p_send.at[s, d], p_recv[s].at[core, source], p_ss.at[s, d], p_rs.at[s, d], sibling).wait_recv()

        b_copy(s, core).start()
        b_copy(s, 1 - core).wait_recv()

    mine = pl.ds(core * chips, chips)
    x_lo, y = me_r // ys, lax.rem(me_r, ys)
    up, down, across = x_lo * ys + lax.rem(y + 1, ys), x_lo * ys + lax.rem(y + ys - 1, ys), (1 - x_lo) * ys + y
    far = x_lo * ys + lax.rem(y + 2, ys)
    far_up, far_down = lax.rem(up + ys, n_rows), lax.rem(down + ys, n_rows)
    far_far = lax.rem(far + ys, n_rows)
    first = pl.ds(core * chips, chips // 2)
    second = pl.ds(core * chips + chips // 2, chips // 2)

    def ag_copy(s, j, slots, source, to):
        block = p_all.at[s, slots, source]
        return remote(block, block, ag_ss.at[s, j], ag_rs.at[s, j], (to, me_c))

    sends = {
        0: (mine, me_r, up), 1: (mine, me_r, down), 2: (mine, me_r, across),
        3: (first, down, up), 4: (second, up, down), 5: (mine, across, up), 6: (mine, across, down), 7: (mine, far, across),
    }
    arrivals = {
        0: (mine, down), 1: (mine, up), 2: (mine, across),
        3: (first, far), 4: (second, far), 5: (mine, far_down), 6: (mine, far_up), 7: (mine, far_far),
    }

    def ag_start(s, j):
        ag_copy(s, j, *sends[j]).start()

    def ag_wait(s, j):
        ag_copy(s, j, *arrivals[j], across).wait_recv()

    def as_copy(s, source, of):
        block = p_all.at[s, pl.ds(of * chips, chips), source]
        return remote(block, block, as_ss.at[s, source], as_rs.at[s, source], sibling)

    def pack(s):
        for t in range(chips):
            k = core * chips + t
            block = p_recv[s][by_k[5, s, chip * n_cols + k], by_k[1, s, chip * n_cols + k]]
            valid = by_k[0, s, chip * n_cols + k] == 1
            p_all[s, k, me_r] = jnp.where(valid, block, jnp.zeros_like(block))

    def ag_first(s):
        for j in (0, 1, 2):
            ag_start(s, j)
        as_copy(s, me_r, core).start()

    def ag_second(s):
        ag_wait(s, 2)
        ag_start(s, 5)
        ag_start(s, 6)
        ag_wait(s, 0)
        ag_start(s, 3)
        ag_wait(s, 1)
        ag_start(s, 4)
        for source in (across, down, up):
            as_copy(s, source, core).start()

    def ag_third(s):
        ag_wait(s, 3)
        ag_wait(s, 4)
        ag_start(s, 7)
        ag_wait(s, 5)
        ag_wait(s, 6)
        for source in (far, far_down, far_up):
            as_copy(s, source, core).start()
        ag_wait(s, 7)
        as_copy(s, far_far, core).start()

    def l_copy(t):
        k = core * chips + t
        return remote(p_all.at[:, k, me_r], l_recv.at[chip], l_ss.at[t], l_rs.at[chip], (me_r, k))

    def l_arrive(j):
        return remote(p_all.at[:, 0, me_r], l_recv.at[j], l_ss.at[0], l_rs.at[j], sibling)

    def l_first():
        @pl.loop(0, chips)
        def _(t):
            k = core * chips + t

            @pl.when(k != me_c)
            def _():
                l_copy(t).start()

            @pl.when(k == me_c)
            def _():
                l_recv[chip] = p_all[:, k, me_r]

    def m_copy(d):
        g = lax.rem(me_r + d, n_rows)
        return remote(l_recv.at[g], left.at[:, me_r], m_ss.at[d], m_rs.at[d], (g, me_c))

    def m_arrive(d):
        source = lax.rem(me_r - d + n_rows, n_rows)
        return remote(l_recv.at[0], left.at[:, source], m_ss.at[d], m_rs.at[d], (source, me_c))

    def l_second():
        @pl.loop(0, chips)
        def _(j):
            @pl.when(2 * j + me_c // chips != me_c)
            def _():
                l_arrive(j).wait_recv()

        left[:, me_r] = l_recv[me_r]

        @pl.loop(1, n_rows)
        def _(d):
            m_copy(d).start()

    to_cores(0)
    pack(0)
    ag_first(0)
    picks(1)
    to_cores(1)
    pack(1)
    ag_second(0)
    ag_first(1)
    l_first()
    ag_third(0)
    ag_second(1)

    def c_copy(s, h):
        return remote(part.at[s, 0, h], core_recv.at[s, h], c_ss.at[s, h], c_rs.at[s, h], sibling)

    def z_copy(s, h, d):
        to = (me_r, (x_hi * zs + lax.rem(z + d, zs)) * 2 + core)
        return remote(z_send.at[s, h, d - 1], z_recv.at[s, h, d - 1], z_ss.at[s, h, d], z_rs.at[s, h, d], to)

    def products(s):
        @pl.loop(0, n_rows)
        def _(source):
            as_copy(s, source, 1 - core).wait_recv()

        @pl.loop(0, 2 * x_his)
        def _(i):
            half_of, h = i // x_his, lax.rem(i + 1 + x_hi, x_his)
            rows = pl.ds(pl.multiple_of((half_of * chips + h * zs) * BS, BS), zs * BS)
            product = jnp.dot(a_pick[s, rows, :], p_all[s].reshape(n_cols * BS, width), preferred_element_type=F32)
            part[s, half_of, h] = product.reshape(zs, BS, width)

            @pl.when(half_of == 0)
            def _():
                c_copy(s, h).start()

        for h in (1 - x_hi, x_hi):
            c_copy(s, h).wait_recv()

            @pl.loop(1, zs)
            def _(d, h=h):
                there = lax.rem(z + d, zs)
                encode(z_send.at[s, h, d - 1], part[s, 1, h, there] + core_recv[s, h, there])
                z_copy(s, h, d).start()

    products(0)
    l_second()
    ag_third(1)
    products(1)

    @pl.loop(1, n_rows)
    def _(d):
        m_arrive(d).wait_recv()

    def x_copy(s):
        to = (me_r, ((1 - x_hi) * zs + z) * 2 + core)
        return remote(x_send.at[s], x_recv.at[s], x_ss.at[s], x_rs.at[s], to)

    def over_z(s, h):
        total = part[s, 1, h, z] + core_recv[s, h, z]
        for d in range(1, zs):
            z_copy(s, h, d).wait_recv()
            total = total + decode(z_recv.at[s, h, d - 1])
        return total

    def start_x(s):
        encode(x_send.at[s], over_z(s, 1 - x_hi))
        x_copy(s).start()

    half = width // 2
    ring = zs
    piece, bit = half // ring, half // ring // ring
    x_at = x_hi * 2 + x_lo

    def ds_copy(s):
        there = pl.ds(pl.multiple_of((1 - core) * half, half), half)
        return remote(d_part.at[s, there], d_sib.at[s], ds_ss.at[s], ds_rs.at[s], sibling)

    def place_in(f, step):
        return y if f == step else z

    def peer_at(f, step, d):
        if step == 2:
            peer = lax.rem(x_at + d, ring)
            return peer, (lax.rem(peer, 2) * ys + y, ((peer // 2) * zs + z) * 2 + core)
        peer = lax.rem(place_in(f, step) + d, ring)
        return peer, (x_lo * ys + peer, me_c) if f == step else (me_r, (x_hi * zs + peer) * 2 + core)

    def u_copy(s, f, d):
        peer, to = peer_at(f, 0, d)
        return remote(u_send.at[s, f, peer], u_recv.at[s, f, d], u_ss.at[s, f, d], u_rs.at[s, f, d], to)

    def v_copy(s, f, d):
        peer, to = peer_at(f, 1, d)
        return remote(v_send.at[s, f, peer], v_recv.at[s, f, d], v_ss.at[s, f, d], v_rs.at[s, f, d], to)

    def t_copy(s, f, d, source):
        block = t_all.at[s, f, source]
        return remote(block, block, t_ss.at[s, f, d], t_rs.at[s, f, d], peer_at(f, 2, d)[1])

    def block_of(s, f, first, rows):
        return diag.at[s, pl.ds(pl.multiple_of(first, rows), rows), f * half : (f + 1) * half]

    def w_copy(s, f, d, source):
        block = block_of(s, f, core * half + place_in(f, 0) * piece + source * bit, bit)
        return remote(block, block, w_ss.at[s, f, d], w_rs.at[s, f, d], peer_at(f, 1, d)[1])

    def er_copy(s, f, d, source):
        block = block_of(s, f, core * half + source * piece, piece)
        return remote(block, block, er_ss.at[s, f, d], er_rs.at[s, f, d], peer_at(f, 0, d)[1])

    def es_copy(s, f, of):
        block = block_of(s, f, of * half, half)
        return remote(block, block, es_ss.at[s, f], es_rs.at[s, f], sibling)

    def finish_sums(s):
        total = over_z(s, x_hi)
        x_copy(s).wait_recv()
        total = total + decode(x_recv.at[s])
        valid = by_k[0, s, me_r * n_cols + me_c] == 1
        total = jnp.where(valid, total, jnp.zeros_like(total))
        out[s] = total
        total = -total
        high = total.astype(BF16)
        low = (total - high.astype(F32)).astype(BF16)
        contract = functools.partial(
            lax.dot_general, dimension_numbers=(((0,), (0,)), ((), ())), preferred_element_type=F32
        )
        for of in (1 - core, core):
            columns = pl.ds(pl.multiple_of(of * half, half), half)
            block = left[s, :, :, columns].reshape(BS, half)
            d_part[s, columns] = contract(block, high) + contract(block, low)
            if of is not core:
                ds_copy(s).start()

    def over_cores(s):
        ds_copy(s).wait_recv()
        here = pl.ds(pl.multiple_of(core * half, half), half)
        total = (d_part[s, here] + d_sib[s]).reshape(ring, piece, width)
        for f in range(2):
            u_send[s, f] = total[:, :, f * half : (f + 1) * half]
            for d in range(1, ring):
                u_copy(s, f, d).start()

    def over_first(s):
        for f in range(2):
            total = u_send[s, f, place_in(f, 0)]
            for d in range(1, ring):
                u_copy(s, f, d).wait_recv()
                total = total + u_recv[s, f, d]
            v_send[s, f] = total.reshape(ring, bit, half)
            for d in range(1, ring):
                v_copy(s, f, d).start()

    def over_second(s):
        for f in range(2):
            total = v_send[s, f, place_in(f, 1)]
            for d in range(1, ring):
                v_copy(s, f, d).wait_recv()
                total = total + v_recv[s, f, d]
            t_all[s, f, x_at] = total
            for d in range(1, ring):
                t_copy(s, f, d, x_at).start()

    def over_third(s):
        for f in range(2):
            for d in range(1, ring):
                t_copy(s, f, d, lax.rem(x_at - d + ring, ring)).wait_recv()
            total = t_all[s, f, 0]
            for x in range(1, ring):
                total = total + t_all[s, f, x]
            first = core * half + place_in(f, 0) * piece + place_in(f, 1) * bit
            diag[s, pl.ds(pl.multiple_of(first, bit), bit), f * half : (f + 1) * half] = total
            for d in range(1, ring):
                w_copy(s, f, d, place_in(f, 1)).start()

    def back_second(s):
        for f in range(2):
            for d in range(1, ring):
                w_copy(s, f, d, lax.rem(place_in(f, 1) - d + ring, ring)).wait_recv()
            for d in range(1, ring):
                er_copy(s, f, d, place_in(f, 0)).start()

    def back_first(s):
        for f in range(2):
            for d in range(1, ring):
                er_copy(s, f, d, lax.rem(place_in(f, 0) - d + ring, ring)).wait_recv()
            es_copy(s, f, core).start()

    start_x(0)
    finish_sums(0)
    over_cores(0)
    start_x(1)
    over_first(0)
    finish_sums(1)
    over_second(0)
    over_cores(1)
    over_third(0)
    over_first(1)
    back_second(0)
    over_second(1)
    back_first(0)
    over_third(1)
    back_second(1)
    back_first(1)

    for s in range(supers):
        @pl.loop(1, n_cols)
        def _(d, s=s):
            p_copy(s, d, me_c).wait_send()

        b_copy(s, core).wait_send()

    @pl.loop(0, chips)
    def _(t):
        @pl.when(core * chips + t != me_c)
        def _():
            l_copy(t).wait_send()

    @pl.loop(1, n_rows)
    def _(d):
        m_copy(d).wait_send()

    for s in range(supers):
        for j in sends:
            ag_copy(s, j, *sends[j]).wait_send()

        @pl.loop(0, n_rows)
        def _(source, s=s):
            as_copy(s, source, core).wait_send()

        for f in range(2):
            for d in range(1, ring):
                u_copy(s, f, d).wait_send()
                v_copy(s, f, d).wait_send()
                t_copy(s, f, d, x_at).wait_send()
                w_copy(s, f, d, place_in(f, 1)).wait_send()
                er_copy(s, f, d, place_in(f, 0)).wait_send()

            es_copy(s, f, core).wait_send()
            es_copy(s, f, 1 - core).wait_recv()

        for h in range(x_his):
            c_copy(s, h).wait_send()
            for d in range(1, zs):
                z_copy(s, h, d).wait_send()
        x_copy(s).wait_send()
        ds_copy(s).wait_send()


def local(n_rows, n_cols, inverse, panels, block_slot, list_ids):
    supers, _, width = panels.shape
    col_blocks = inverse.shape[1] // BS
    sub = BS // n_rows
    x_his = 2
    chips = n_cols // 2
    zs = chips // x_his
    half = width // 2
    lists = tables(block_slot, list_ids, n_rows, n_cols)
    blocks = inverse.reshape(-1, BS, inverse.shape[1])
    vmem = pl.BlockSpec(memory_space=pltpu.VMEM)
    smem = pl.BlockSpec(memory_space=pltpu.SMEM)
    dma = pltpu.SemaphoreType.DMA
    scratch = [
        pltpu.VMEM((col_blocks, blocks.shape[0], BS, BS), BF16),
        pltpu.VMEM((supers, n_cols * BS, n_cols * BS), BF16),
        pltpu.VMEM((supers, n_cols, sub, width), BF16),
        pltpu.VMEM((2, n_cols, sub, width), BF16),
        pltpu.VMEM((2, n_cols, sub, width), BF16),
        pltpu.VMEM((supers, n_cols, n_rows, sub, width), BF16),
        pltpu.VMEM((chips, supers, sub, width), BF16),
        pltpu.VMEM((supers, n_rows, sub, width), BF16),
        pltpu.VMEM((supers, 2, x_his, zs, BS, width), F32),
        pltpu.VMEM((supers, x_his, zs, BS, width), F32),
        pltpu.VMEM((supers, x_his, zs - 1, BS + SCALE_ROWS, width), jnp.int16),
        pltpu.VMEM((supers, x_his, zs - 1, BS + SCALE_ROWS, width), jnp.int16),
        pltpu.VMEM((supers, BS + SCALE_ROWS, width), jnp.int16),
        pltpu.VMEM((supers, BS + SCALE_ROWS, width), jnp.int16),
        pltpu.VMEM((supers, width, width), F32),
        pltpu.VMEM((supers, half, width), F32),
        pltpu.VMEM((supers, 2, zs, half // zs, half), F32),
        pltpu.VMEM((supers, 2, zs, half // zs, half), F32),
        pltpu.VMEM((supers, 2, zs, half // zs // zs, half), F32),
        pltpu.VMEM((supers, 2, zs, half // zs // zs, half), F32),
        pltpu.VMEM((supers, 2, zs, half // zs // zs, half), F32),
        dma((col_blocks,)),
        dma((supers, n_cols)), dma((supers, n_cols)),
        dma((supers,)), dma((supers,)),
        dma((supers, 8)), dma((supers, 8)),
        dma((supers, n_rows)), dma((supers, n_rows)),
        dma((chips,)), dma((chips,)),
        dma((n_rows,)), dma((n_rows,)),
        dma((supers, x_his)), dma((supers, x_his)),
        dma((supers, x_his, zs)), dma((supers, x_his, zs)),
        dma((supers,)), dma((supers,)),
        dma((supers,)), dma((supers,)),
        dma((supers, 2, zs)), dma((supers, 2, zs)),
        dma((supers, 2, zs)), dma((supers, 2, zs)),
        dma((supers, 2, zs)), dma((supers, 2, zs)),
        dma((supers, 2, zs)), dma((supers, 2, zs)),
        dma((supers, 2, zs)), dma((supers, 2, zs)),
        dma((supers, 2)), dma((supers, 2)),
    ]
    return pl.pallas_call(
        functools.partial(kernel, n_rows, n_cols, x_his),
        out_shape=(
            jax.ShapeDtypeStruct((supers, BS, width), F32),
            jax.ShapeDtypeStruct((supers, width, width), F32),
        ),
        in_specs=[pl.BlockSpec(memory_space=pl.ANY), vmem, smem, smem],
        out_specs=(vmem, vmem),
        scratch_shapes=scratch,
        compiler_params=pltpu.CompilerParams(
            collective_id=0, has_side_effects=True, vmem_limit_bytes=60 * 2**20
        ),
    )(blocks, panels, *lists)


def solution(mesh):
    n_rows, n_cols = mesh.shape["row"], mesh.shape["col"]
    return jax.shard_map(
        functools.partial(local, n_rows, n_cols),
        mesh=mesh,
        in_specs=(P("row", "col"), P(None, "col", None), P(), P()),
        out_specs=(P(None, ("row", "col"), None), P()),
        check_vma=False,
    )
```

```python
import functools

import jax
import jax.numpy as jnp
from jax import lax
from jax.experimental import pallas as pl
from jax.experimental.pallas import tpu as pltpu
from jax.sharding import PartitionSpec as P

BS = 128
MESH = pl.DeviceIdType.MESH
F32 = jnp.float32
BF16 = jnp.bfloat16


def tables(block_slot, list_ids, n_rows, n_cols):
    n_blocks, listed = block_slot.shape[0], list_ids.shape[1]
    ids = jnp.arange(n_blocks, dtype=jnp.int32)
    slots = jnp.sum(jnp.where(list_ids[..., None] == ids, block_slot, 0), axis=-1)
    col_blocks, row_blocks = n_blocks // n_cols, n_blocks // n_rows
    row = slots // row_blocks
    pos = jnp.arange(listed, dtype=jnp.int32)
    before = pos[None, :] < pos[:, None]
    kth = jnp.sum(((row[:, :, None] == row[:, None, :]) & before).astype(jnp.int32), axis=-1)
    key = row * n_cols + kth
    keys = jnp.arange(n_rows * n_cols, dtype=jnp.int32)
    code = jnp.sum(jnp.where(key[:, None, :] == keys[:, None], (1 + slots * listed + pos)[:, None, :], 0), axis=-1)
    slot, place = jnp.maximum(code - 1, 0) // listed, jnp.maximum(code - 1, 0) % listed
    shard = listed // n_cols
    table = jnp.stack(
        [
            (code > 0).astype(jnp.int32), place // shard, slot // col_blocks, slot % col_blocks, slot % row_blocks,
            slot // col_blocks % 2,
        ]
    )
    return slots // col_blocks, table


SCALE_ROWS = 16
TOP = 32000.0


def encode(ref, block):
    top = jnp.max(jnp.abs(block), axis=0, keepdims=True)
    exponent = jnp.floor(jnp.log2(jnp.maximum(top, 1e-30))) + 1.0
    coded = jnp.round(block * (jnp.exp2(-exponent) * TOP))
    ref[0:BS] = coded.astype(jnp.int32).astype(jnp.int16)
    exponents = jnp.broadcast_to(exponent, (SCALE_ROWS, block.shape[1]))
    ref[BS : BS + SCALE_ROWS] = exponents.astype(jnp.int32).astype(jnp.int16)


def decode(ref):
    exponent = ref[BS : BS + SCALE_ROWS].astype(jnp.int32).astype(F32)[0:1]
    return ref[0:BS].astype(jnp.int32).astype(F32) * (jnp.exp2(exponent) * (1.0 / TOP))


def kernel(
    n_rows, n_cols, x_his,
    inv_hbm, pan, cols, by_k,
    out, diag,
    a_all, a_pick, p_send, p_recv_0, p_recv_1, p_all, l_recv, left,
    part, core_recv, z_send, z_recv, x_send, x_recv, d_part, d_sib, u_send, u_recv, v_send, v_recv, t_all,
    a_sem, p_ss, p_rs, b_ss, b_rs, ag_ss, ag_rs, as_ss, as_rs, l_ss, l_rs, m_ss, m_rs, c_ss, c_rs, z_ss, z_rs, x_ss, x_rs,
    ds_ss, ds_rs, u_ss, u_rs, v_ss, v_rs, t_ss, t_rs, w_ss, w_rs, er_ss, er_rs, es_ss, es_rs,
):
    supers = pan.shape[0]
    p_recv = (p_recv_0, p_recv_1)
    sub = BS // n_rows
    col_blocks = a_all.shape[0]
    shard = pan.shape[1] // BS
    width = pan.shape[2]
    chips = n_cols // 2
    zs = chips // x_his
    ys = n_rows // 2
    me_r, me_c = lax.axis_index("row"), lax.axis_index("col")
    core = lax.rem(me_c, 2)
    chip = me_c // 2
    x_hi, z = chip // zs, lax.rem(chip, zs)
    sibling = (me_r, me_c + 1 - 2 * core)

    def remote(src, dst, ss, rs, to):
        return pltpu.make_async_remote_copy(
            src_ref=src, dst_ref=dst, send_sem=ss, recv_sem=rs, device_id=to, device_id_type=MESH
        )

    def load_a(b):
        columns = pl.ds(pl.multiple_of(b * BS, BS), BS)
        return pltpu.make_async_copy(inv_hbm.at[:, :, columns], a_all.at[b], a_sem.at[b])

    @pl.loop(0, col_blocks)
    def _(b):
        load_a(b).start()

    barrier = pltpu.get_barrier_semaphore()

    @pl.loop(1, n_cols)
    def _(d):
        pl.semaphore_signal(barrier, inc=1, device_id=(me_r, lax.rem(me_c + d, n_cols)), device_id_type=MESH)

    @pl.loop(1, n_rows)
    def _(d):
        pl.semaphore_signal(barrier, inc=1, device_id=(lax.rem(me_r + d, n_rows), me_c), device_id_type=MESH)

    opposite = (lax.rem(me_r + ys, n_rows), lax.rem(me_c + zs * 2, n_cols))
    pl.semaphore_signal(barrier, inc=1, device_id=opposite, device_id_type=MESH)

    def pick_for(c, s):
        piece = jnp.zeros((sub, width), BF16)
        for q in range(shard):
            block = pan[s, pl.ds(pl.multiple_of(q * BS + me_r * sub, sub), sub), :]
            piece = jnp.where(cols[s, me_c * shard + q] == c, block, piece)
        return piece

    @pl.loop(1, n_cols)
    def _(d):
        for s in range(supers):
            p_send[s, d] = pick_for(lax.rem(me_c + d, n_cols), s)

    for s in range(supers):
        p_recv[s][core, me_c] = pick_for(me_c, s)

    pl.semaphore_wait(barrier, n_cols + n_rows - 1)

    def p_copy(s, d, source):
        to = (me_r, lax.rem(me_c + d, n_cols))
        return remote(p_send.at[s, d], p_recv[s].at[lax.rem(to[1], 2), source], p_ss.at[s, d], p_rs.at[s, d], to)

    for s in range(supers):
        @pl.loop(1, n_cols)
        def _(d, s=s):
            p_copy(s, d, me_c).start()

    def picks(s):
        @pl.loop(0, n_cols)
        def _(i):
            half_of, place = i // chips, lax.rem(i, chips)
            k = 2 * place + jnp.where(half_of == 1, core, 1 - core)
            a_row = by_k[4, s, me_r * n_cols + k]
            rows = pl.ds(pl.multiple_of(i * BS, BS), BS)
            for b in range(n_cols):
                block = a_all[by_k[3, s, chip * n_cols + b], a_row]
                here = by_k[0, s, chip * n_cols + b] * (by_k[2, s, chip * n_cols + b] == me_c) == 1
                a_pick[s, rows, b * BS : (b + 1) * BS] = jnp.where(here, block, jnp.zeros_like(block))

    @pl.loop(0, col_blocks)
    def _(b):
        load_a(b).wait()

    picks(0)

    def b_copy(s, of):
        return remote(p_recv[s].at[of], p_recv[s].at[of], b_ss.at[s], b_rs.at[s], sibling)

    def to_cores(s):
        @pl.loop(1, n_cols)
        def _(d):
            source = lax.rem(me_c - d + n_cols, n_cols)
            remote(p_send.at[s, d], p_recv[s].at[core, source], p_ss.at[s, d], p_rs.at[s, d], sibling).wait_recv()

        b_copy(s, core).start()

    mine = pl.ds(core * chips, chips)
    x_lo, y = me_r // ys, lax.rem(me_r, ys)
    up, down, across = x_lo * ys + lax.rem(y + 1, ys), x_lo * ys + lax.rem(y + ys - 1, ys), (1 - x_lo) * ys + y
    far = x_lo * ys + lax.rem(y + 2, ys)
    far_up, far_down = lax.rem(up + ys, n_rows), lax.rem(down + ys, n_rows)
    far_far = lax.rem(far + ys, n_rows)
    first = pl.ds(core * chips, chips // 2)
    second = pl.ds(core * chips + chips // 2, chips // 2)

    def ag_copy(s, j, slots, source, to):
        block = p_all.at[s, slots, source]
        return remote(block, block, ag_ss.at[s, j], ag_rs.at[s, j], (to, me_c))

    sends = {
        0: (mine, me_r, up), 1: (mine, me_r, down), 2: (mine, me_r, across),
        3: (first, down, up), 4: (second, up, down), 5: (mine, across, up), 6: (mine, across, down), 7: (mine, far, across),
    }
    arrivals = {
        0: (mine, down), 1: (mine, up), 2: (mine, across),
        3: (first, far), 4: (second, far), 5: (mine, far_down), 6: (mine, far_up), 7: (mine, far_far),
    }

    def ag_start(s, j):
        ag_copy(s, j, *sends[j]).start()

    def ag_wait(s, j):
        ag_copy(s, j, *arrivals[j], across).wait_recv()

    def as_copy(s, source, of):
        block = p_all.at[s, pl.ds(of * chips, chips), source]
        return remote(block, block, as_ss.at[s, source], as_rs.at[s, source], sibling)

    def pack(s):
        b_copy(s, 1 - core).wait_recv()
        for t in range(chips):
            k = core * chips + t
            block = p_recv[s][by_k[5, s, chip * n_cols + k], by_k[1, s, chip * n_cols + k]]
            valid = by_k[0, s, chip * n_cols + k] == 1
            p_all[s, k, me_r] = jnp.where(valid, block, jnp.zeros_like(block))

    def ag_first(s):
        for j in (0, 1, 2):
            ag_start(s, j)
        as_copy(s, me_r, core).start()

    def ag_second(s):
        ag_wait(s, 2)
        ag_start(s, 5)
        ag_start(s, 6)
        ag_wait(s, 0)
        ag_start(s, 3)
        ag_wait(s, 1)
        ag_start(s, 4)
        for source in (across, down, up):
            as_copy(s, source, core).start()

    def ag_third(s):
        ag_wait(s, 3)
        ag_wait(s, 4)
        ag_start(s, 7)
        ag_wait(s, 5)
        ag_wait(s, 6)
        for source in (far, far_down, far_up):
            as_copy(s, source, core).start()
        ag_wait(s, 7)
        as_copy(s, far_far, core).start()

    def l_copy(t):
        k = core * chips + t
        return remote(p_all.at[:, k, me_r], l_recv.at[chip], l_ss.at[t], l_rs.at[chip], (me_r, k))

    def l_arrive(j):
        return remote(p_all.at[:, 0, me_r], l_recv.at[j], l_ss.at[0], l_rs.at[j], sibling)

    def l_first():
        @pl.loop(0, chips)
        def _(t):
            k = core * chips + t

            @pl.when(k != me_c)
            def _():
                l_copy(t).start()

            @pl.when(k == me_c)
            def _():
                l_recv[chip] = p_all[:, k, me_r]

    def m_copy(d):
        g = lax.rem(me_r + d, n_rows)
        return remote(l_recv.at[g], left.at[:, me_r], m_ss.at[d], m_rs.at[d], (g, me_c))

    def m_arrive(d):
        source = lax.rem(me_r - d + n_rows, n_rows)
        return remote(l_recv.at[0], left.at[:, source], m_ss.at[d], m_rs.at[d], (source, me_c))

    def l_second():
        @pl.loop(0, chips)
        def _(j):
            @pl.when(2 * j + me_c // chips != me_c)
            def _():
                l_arrive(j).wait_recv()

        left[:, me_r] = l_recv[me_r]

        @pl.loop(1, n_rows)
        def _(d):
            m_copy(d).start()

    to_cores(0)
    pack(0)
    ag_first(0)
    picks(1)
    to_cores(1)
    ag_second(0)
    pack(1)
    ag_first(1)
    l_first()
    ag_third(0)
    ag_second(1)

    def c_copy(s, h):
        return remote(part.at[s, 0, h], core_recv.at[s, h], c_ss.at[s, h], c_rs.at[s, h], sibling)

    def z_copy(s, h, d):
        to = (me_r, (x_hi * zs + lax.rem(z + d, zs)) * 2 + core)
        return remote(z_send.at[s, h, d - 1], z_recv.at[s, h, d - 1], z_ss.at[s, h, d], z_rs.at[s, h, d], to)

    def products(s):
        @pl.loop(0, n_rows)
        def _(source):
            as_copy(s, source, 1 - core).wait_recv()

        def product(half_of, h):
            rows = pl.ds(pl.multiple_of((half_of * chips + h * zs) * BS, BS), zs * BS)
            result = jnp.dot(a_pick[s, rows, :], p_all[s].reshape(n_cols * BS, width), preferred_element_type=F32)
            part[s, half_of, h] = result.reshape(zs, BS, width)

        def to_z(h):
            c_copy(s, h).wait_recv()

            @pl.loop(1, zs)
            def _(d):
                there = lax.rem(z + d, zs)
                encode(z_send.at[s, h, d - 1], part[s, 1, h, there] + core_recv[s, h, there])
                z_copy(s, h, d).start()

        @pl.loop(0, x_his)
        def _(step):
            h = jnp.where(step == 0, 1 - x_hi, x_hi)
            product(0, h)
            c_copy(s, h).start()

            @pl.when(step > 0)
            def _():
                to_z(1 - x_hi)

            product(1, h)

        to_z(x_hi)

    products(0)
    l_second()
    ag_third(1)
    products(1)

    @pl.loop(1, n_rows)
    def _(d):
        m_arrive(d).wait_recv()

    def x_copy(s):
        to = (me_r, ((1 - x_hi) * zs + z) * 2 + core)
        return remote(x_send.at[s], x_recv.at[s], x_ss.at[s], x_rs.at[s], to)

    def over_z(s, h):
        total = part[s, 1, h, z] + core_recv[s, h, z]
        for d in range(1, zs):
            z_copy(s, h, d).wait_recv()
            total = total + decode(z_recv.at[s, h, d - 1])
        return total

    def start_x(s):
        encode(x_send.at[s], over_z(s, 1 - x_hi))
        x_copy(s).start()

    half = width // 2
    ring = zs
    piece, bit = half // ring, half // ring // ring
    x_at = x_hi * 2 + x_lo

    def ds_copy(s):
        there = pl.ds(pl.multiple_of((1 - core) * half, half), half)
        return remote(d_part.at[s, there], d_sib.at[s], ds_ss.at[s], ds_rs.at[s], sibling)

    def place_in(f, step):
        return y if f == step else z

    def peer_at(f, step, d):
        if step == 2:
            peer = lax.rem(x_at + d, ring)
            return peer, (lax.rem(peer, 2) * ys + y, ((peer // 2) * zs + z) * 2 + core)
        peer = lax.rem(place_in(f, step) + d, ring)
        return peer, (x_lo * ys + peer, me_c) if f == step else (me_r, (x_hi * zs + peer) * 2 + core)

    def u_copy(s, f, d):
        peer, to = peer_at(f, 0, d)
        return remote(u_send.at[s, f, peer], u_recv.at[s, f, d], u_ss.at[s, f, d], u_rs.at[s, f, d], to)

    def v_copy(s, f, d):
        peer, to = peer_at(f, 1, d)
        return remote(v_send.at[s, f, peer], v_recv.at[s, f, d], v_ss.at[s, f, d], v_rs.at[s, f, d], to)

    def t_copy(s, f, d, source):
        block = t_all.at[s, f, source]
        return remote(block, block, t_ss.at[s, f, d], t_rs.at[s, f, d], peer_at(f, 2, d)[1])

    def block_of(s, f, first, rows):
        return diag.at[s, pl.ds(pl.multiple_of(first, rows), rows), f * half : (f + 1) * half]

    def w_copy(s, f, d, source):
        block = block_of(s, f, core * half + place_in(f, 0) * piece + source * bit, bit)
        return remote(block, block, w_ss.at[s, f, d], w_rs.at[s, f, d], peer_at(f, 1, d)[1])

    def er_copy(s, f, d, source):
        block = block_of(s, f, core * half + source * piece, piece)
        return remote(block, block, er_ss.at[s, f, d], er_rs.at[s, f, d], peer_at(f, 0, d)[1])

    def es_copy(s, f, of):
        block = block_of(s, f, of * half, half)
        return remote(block, block, es_ss.at[s, f], es_rs.at[s, f], sibling)

    def finish_sums(s):
        total = over_z(s, x_hi)
        x_copy(s).wait_recv()
        total = total + decode(x_recv.at[s])
        valid = by_k[0, s, me_r * n_cols + me_c] == 1
        total = jnp.where(valid, total, jnp.zeros_like(total))
        out[s] = total
        total = -total
        high = total.astype(BF16)
        low = (total - high.astype(F32)).astype(BF16)
        contract = functools.partial(
            lax.dot_general, dimension_numbers=(((0,), (0,)), ((), ())), preferred_element_type=F32
        )
        for of in (1 - core, core):
            columns = pl.ds(pl.multiple_of(of * half, half), half)
            block = left[s, :, :, columns].reshape(BS, half)
            d_part[s, columns] = contract(block, high) + contract(block, low)
            if of is not core:
                ds_copy(s).start()

    def over_cores(s):
        ds_copy(s).wait_recv()
        here = pl.ds(pl.multiple_of(core * half, half), half)
        total = (d_part[s, here] + d_sib[s]).reshape(ring, piece, width)
        for f in range(2):
            u_send[s, f] = total[:, :, f * half : (f + 1) * half]
            for d in range(1, ring):
                u_copy(s, f, d).start()

    def over_first(s):
        for f in range(2):
            total = u_send[s, f, place_in(f, 0)]
            for d in range(1, ring):
                u_copy(s, f, d).wait_recv()
                total = total + u_recv[s, f, d]
            v_send[s, f] = total.reshape(ring, bit, half)
            for d in range(1, ring):
                v_copy(s, f, d).start()

    def over_second(s):
        for f in range(2):
            total = v_send[s, f, place_in(f, 1)]
            for d in range(1, ring):
                v_copy(s, f, d).wait_recv()
                total = total + v_recv[s, f, d]
            t_all[s, f, x_at] = total
            for d in range(1, ring):
                t_copy(s, f, d, x_at).start()

    def over_third(s):
        for f in range(2):
            for d in range(1, ring):
                t_copy(s, f, d, lax.rem(x_at - d + ring, ring)).wait_recv()
            total = t_all[s, f, 0]
            for x in range(1, ring):
                total = total + t_all[s, f, x]
            first = core * half + place_in(f, 0) * piece + place_in(f, 1) * bit
            diag[s, pl.ds(pl.multiple_of(first, bit), bit), f * half : (f + 1) * half] = total
            for d in range(1, ring):
                w_copy(s, f, d, place_in(f, 1)).start()

    def back_second(s):
        for f in range(2):
            for d in range(1, ring):
                w_copy(s, f, d, lax.rem(place_in(f, 1) - d + ring, ring)).wait_recv()
            for d in range(1, ring):
                er_copy(s, f, d, place_in(f, 0)).start()

    def back_first(s):
        for f in range(2):
            for d in range(1, ring):
                er_copy(s, f, d, lax.rem(place_in(f, 0) - d + ring, ring)).wait_recv()
            es_copy(s, f, core).start()

    start_x(0)
    finish_sums(0)
    over_cores(0)
    start_x(1)
    over_first(0)
    finish_sums(1)
    over_second(0)
    over_cores(1)
    over_third(0)
    over_first(1)
    back_second(0)
    over_second(1)
    back_first(0)
    over_third(1)
    back_second(1)
    back_first(1)

    for s in range(supers):
        @pl.loop(1, n_cols)
        def _(d, s=s):
            p_copy(s, d, me_c).wait_send()

        b_copy(s, core).wait_send()

    @pl.loop(0, chips)
    def _(t):
        @pl.when(core * chips + t != me_c)
        def _():
            l_copy(t).wait_send()

    @pl.loop(1, n_rows)
    def _(d):
        m_copy(d).wait_send()

    for s in range(supers):
        for j in sends:
            ag_copy(s, j, *sends[j]).wait_send()

        @pl.loop(0, n_rows)
        def _(source, s=s):
            as_copy(s, source, core).wait_send()

        for f in range(2):
            for d in range(1, ring):
                u_copy(s, f, d).wait_send()
                v_copy(s, f, d).wait_send()
                t_copy(s, f, d, x_at).wait_send()
                w_copy(s, f, d, place_in(f, 1)).wait_send()
                er_copy(s, f, d, place_in(f, 0)).wait_send()

            es_copy(s, f, core).wait_send()
            es_copy(s, f, 1 - core).wait_recv()

        for h in range(x_his):
            c_copy(s, h).wait_send()
            for d in range(1, zs):
                z_copy(s, h, d).wait_send()
        x_copy(s).wait_send()
        ds_copy(s).wait_send()


def local(n_rows, n_cols, inverse, panels, block_slot, list_ids):
    supers, _, width = panels.shape
    col_blocks = inverse.shape[1] // BS
    sub = BS // n_rows
    x_his = 2
    chips = n_cols // 2
    zs = chips // x_his
    half = width // 2
    lists = tables(block_slot, list_ids, n_rows, n_cols)
    blocks = inverse.reshape(-1, BS, inverse.shape[1])
    vmem = pl.BlockSpec(memory_space=pltpu.VMEM)
    smem = pl.BlockSpec(memory_space=pltpu.SMEM)
    dma = pltpu.SemaphoreType.DMA
    scratch = [
        pltpu.VMEM((col_blocks, blocks.shape[0], BS, BS), BF16),
        pltpu.VMEM((supers, n_cols * BS, n_cols * BS), BF16),
        pltpu.VMEM((supers, n_cols, sub, width), BF16),
        pltpu.VMEM((2, n_cols, sub, width), BF16),
        pltpu.VMEM((2, n_cols, sub, width), BF16),
        pltpu.VMEM((supers, n_cols, n_rows, sub, width), BF16),
        pltpu.VMEM((chips, supers, sub, width), BF16),
        pltpu.VMEM((supers, n_rows, sub, width), BF16),
        pltpu.VMEM((supers, 2, x_his, zs, BS, width), F32),
        pltpu.VMEM((supers, x_his, zs, BS, width), F32),
        pltpu.VMEM((supers, x_his, zs - 1, BS + SCALE_ROWS, width), jnp.int16),
        pltpu.VMEM((supers, x_his, zs - 1, BS + SCALE_ROWS, width), jnp.int16),
        pltpu.VMEM((supers, BS + SCALE_ROWS, width), jnp.int16),
        pltpu.VMEM((supers, BS + SCALE_ROWS, width), jnp.int16),
        pltpu.VMEM((supers, width, width), F32),
        pltpu.VMEM((supers, half, width), F32),
        pltpu.VMEM((supers, 2, zs, half // zs, half), F32),
        pltpu.VMEM((supers, 2, zs, half // zs, half), F32),
        pltpu.VMEM((supers, 2, zs, half // zs // zs, half), F32),
        pltpu.VMEM((supers, 2, zs, half // zs // zs, half), F32),
        pltpu.VMEM((supers, 2, zs, half // zs // zs, half), F32),
        dma((col_blocks,)),
        dma((supers, n_cols)), dma((supers, n_cols)),
        dma((supers,)), dma((supers,)),
        dma((supers, 8)), dma((supers, 8)),
        dma((supers, n_rows)), dma((supers, n_rows)),
        dma((chips,)), dma((chips,)),
        dma((n_rows,)), dma((n_rows,)),
        dma((supers, x_his)), dma((supers, x_his)),
        dma((supers, x_his, zs)), dma((supers, x_his, zs)),
        dma((supers,)), dma((supers,)),
        dma((supers,)), dma((supers,)),
        dma((supers, 2, zs)), dma((supers, 2, zs)),
        dma((supers, 2, zs)), dma((supers, 2, zs)),
        dma((supers, 2, zs)), dma((supers, 2, zs)),
        dma((supers, 2, zs)), dma((supers, 2, zs)),
        dma((supers, 2, zs)), dma((supers, 2, zs)),
        dma((supers, 2)), dma((supers, 2)),
    ]
    return pl.pallas_call(
        functools.partial(kernel, n_rows, n_cols, x_his),
        out_shape=(
            pltpu.VMEM((supers, BS, width), F32),
            pltpu.VMEM((supers, width, width), F32),
        ),
        in_specs=[pl.BlockSpec(memory_space=pl.ANY), vmem, smem, smem],
        out_specs=(vmem, vmem),
        scratch_shapes=scratch,
        compiler_params=pltpu.CompilerParams(
            collective_id=0, has_side_effects=True, vmem_limit_bytes=60 * 2**20
        ),
    )(blocks, panels, *lists)


def solution(mesh):
    n_rows, n_cols = mesh.shape["row"], mesh.shape["col"]
    return jax.shard_map(
        functools.partial(local, n_rows, n_cols),
        mesh=mesh,
        in_specs=(P("row", "col"), P(None, "col", None), P(), P()),
        out_specs=(P(None, ("row", "col"), None), P()),
        check_vma=False,
    )
```

```python
import functools

import jax
import jax.numpy as jnp
from jax import lax
from jax.experimental import pallas as pl
from jax.experimental.pallas import tpu as pltpu
from jax.sharding import PartitionSpec as P

BS = 128
MESH = pl.DeviceIdType.MESH
F32 = jnp.float32
BF16 = jnp.bfloat16


def tables(block_slot, list_ids, n_rows, n_cols):
    n_blocks, listed = block_slot.shape[0], list_ids.shape[1]
    ids = jnp.arange(n_blocks, dtype=jnp.int32)
    slots = jnp.sum(jnp.where(list_ids[..., None] == ids, block_slot, 0), axis=-1)
    col_blocks, row_blocks = n_blocks // n_cols, n_blocks // n_rows
    row = slots // row_blocks
    pos = jnp.arange(listed, dtype=jnp.int32)
    before = pos[None, :] < pos[:, None]
    kth = jnp.sum(((row[:, :, None] == row[:, None, :]) & before).astype(jnp.int32), axis=-1)
    key = row * n_cols + kth
    keys = jnp.arange(n_rows * n_cols, dtype=jnp.int32)
    code = jnp.sum(jnp.where(key[:, None, :] == keys[:, None], (1 + slots * listed + pos)[:, None, :], 0), axis=-1)
    slot, place = jnp.maximum(code - 1, 0) // listed, jnp.maximum(code - 1, 0) % listed
    shard = listed // n_cols
    table = jnp.stack(
        [
            (code > 0).astype(jnp.int32), place // shard, slot // col_blocks, slot % col_blocks, slot % row_blocks,
            slot // col_blocks % 2,
        ]
    )
    return slots // col_blocks, table


SCALE_ROWS = 16
TOP = 32000.0


def encode(ref, block):
    top = jnp.max(jnp.abs(block), axis=0, keepdims=True)
    exponent = jnp.floor(jnp.log2(jnp.maximum(top, 1e-30))) + 1.0
    coded = jnp.round(block * (jnp.exp2(-exponent) * TOP))
    ref[0:BS] = coded.astype(jnp.int32).astype(jnp.int16)
    exponents = jnp.broadcast_to(exponent, (SCALE_ROWS, block.shape[1]))
    ref[BS : BS + SCALE_ROWS] = exponents.astype(jnp.int32).astype(jnp.int16)


def decode(ref):
    exponent = ref[BS : BS + SCALE_ROWS].astype(jnp.int32).astype(F32)[0:1]
    return ref[0:BS].astype(jnp.int32).astype(F32) * (jnp.exp2(exponent) * (1.0 / TOP))


def kernel(
    n_rows, n_cols, x_his,
    inv_hbm, pan_hbm, cols, by_k,
    out, diag,
    pan, a_all, a_pick, p_send, p_recv_0, p_recv_1, p_all, l_recv, left,
    part, core_recv, z_send, z_recv, x_send, x_recv, d_part, d_sib, u_send, u_recv, v_send, v_recv, t_all,
    pan_sem, a_sem, p_ss, p_rs, b_ss, b_rs, ag_ss, ag_rs, as_ss, as_rs, l_ss, l_rs, m_ss, m_rs, c_ss, c_rs, z_ss, z_rs, x_ss, x_rs,
    ds_ss, ds_rs, u_ss, u_rs, v_ss, v_rs, t_ss, t_rs, w_ss, w_rs, er_ss, er_rs, es_ss, es_rs,
):
    supers = pan.shape[0]
    p_recv = (p_recv_0, p_recv_1)
    sub = BS // n_rows
    col_blocks = a_all.shape[0]
    shard = pan.shape[1]
    width = pan.shape[3]
    chips = n_cols // 2
    zs = chips // x_his
    ys = n_rows // 2
    me_r, me_c = lax.axis_index("row"), lax.axis_index("col")
    core = lax.rem(me_c, 2)
    chip = me_c // 2
    x_hi, z = chip // zs, lax.rem(chip, zs)
    sibling = (me_r, me_c + 1 - 2 * core)

    def remote(src, dst, ss, rs, to):
        return pltpu.make_async_remote_copy(
            src_ref=src, dst_ref=dst, send_sem=ss, recv_sem=rs, device_id=to, device_id_type=MESH
        )

    barrier = pltpu.get_barrier_semaphore()

    @pl.loop(1, n_cols)
    def _(d):
        pl.semaphore_signal(barrier, inc=1, device_id=(me_r, lax.rem(me_c + d, n_cols)), device_id_type=MESH)

    @pl.loop(1, n_rows)
    def _(d):
        pl.semaphore_signal(barrier, inc=1, device_id=(lax.rem(me_r + d, n_rows), me_c), device_id_type=MESH)

    opposite = (lax.rem(me_r + ys, n_rows), lax.rem(me_c + zs * 2, n_cols))
    pl.semaphore_signal(barrier, inc=1, device_id=opposite, device_id_type=MESH)

    load_pan = pltpu.make_async_copy(pan_hbm.at[:, :, me_r], pan, pan_sem)
    load_pan.start()

    def load_a(b):
        columns = pl.ds(pl.multiple_of(b * BS, BS), BS)
        return pltpu.make_async_copy(inv_hbm.at[:, :, columns], a_all.at[b], a_sem.at[b])

    @pl.loop(0, col_blocks)
    def _(b):
        load_a(b).start()

    load_pan.wait()

    def pick_for(c, s):
        piece = jnp.zeros((sub, width), BF16)
        for q in range(shard):
            piece = jnp.where(cols[s, me_c * shard + q] == c, pan[s, q], piece)
        return piece

    @pl.loop(1, n_cols)
    def _(d):
        for s in range(supers):
            p_send[s, d] = pick_for(lax.rem(me_c + d, n_cols), s)

    for s in range(supers):
        p_recv[s][core, me_c] = pick_for(me_c, s)

    pl.semaphore_wait(barrier, n_cols + n_rows - 1)

    def p_copy(s, d, source):
        to = (me_r, lax.rem(me_c + d, n_cols))
        return remote(p_send.at[s, d], p_recv[s].at[lax.rem(to[1], 2), source], p_ss.at[s, d], p_rs.at[s, d], to)

    for s in range(supers):
        @pl.loop(1, n_cols)
        def _(d, s=s):
            p_copy(s, d, me_c).start()

    def picks(s):
        @pl.loop(0, n_cols)
        def _(i):
            half_of, place = i // chips, lax.rem(i, chips)
            k = 2 * place + jnp.where(half_of == 1, core, 1 - core)
            a_row = by_k[4, s, me_r * n_cols + k]
            rows = pl.ds(pl.multiple_of(i * BS, BS), BS)
            for b in range(n_cols):
                block = a_all[by_k[3, s, chip * n_cols + b], a_row]
                here = by_k[0, s, chip * n_cols + b] * (by_k[2, s, chip * n_cols + b] == me_c) == 1
                a_pick[s, rows, b * BS : (b + 1) * BS] = jnp.where(here, block, jnp.zeros_like(block))

    @pl.loop(0, col_blocks)
    def _(b):
        load_a(b).wait()

    picks(0)

    def b_copy(s, of):
        return remote(p_recv[s].at[of], p_recv[s].at[of], b_ss.at[s], b_rs.at[s], sibling)

    def to_cores(s):
        @pl.loop(1, n_cols)
        def _(d):
            source = lax.rem(me_c - d + n_cols, n_cols)
            remote(p_send.at[s, d], p_recv[s].at[core, source], p_ss.at[s, d], p_rs.at[s, d], sibling).wait_recv()

        b_copy(s, core).start()

    mine = pl.ds(core * chips, chips)
    x_lo, y = me_r // ys, lax.rem(me_r, ys)
    up, down, across = x_lo * ys + lax.rem(y + 1, ys), x_lo * ys + lax.rem(y + ys - 1, ys), (1 - x_lo) * ys + y
    far = x_lo * ys + lax.rem(y + 2, ys)
    far_up, far_down = lax.rem(up + ys, n_rows), lax.rem(down + ys, n_rows)
    far_far = lax.rem(far + ys, n_rows)
    first = pl.ds(core * chips, chips // 2)
    second = pl.ds(core * chips + chips // 2, chips // 2)

    def ag_copy(s, j, slots, source, to):
        block = p_all.at[s, slots, source]
        return remote(block, block, ag_ss.at[s, j], ag_rs.at[s, j], (to, me_c))

    sends = {
        0: (mine, me_r, up), 1: (mine, me_r, down), 2: (mine, me_r, across),
        3: (first, down, up), 4: (second, up, down), 5: (mine, across, up), 6: (mine, across, down), 7: (mine, far, across),
    }
    arrivals = {
        0: (mine, down), 1: (mine, up), 2: (mine, across),
        3: (first, far), 4: (second, far), 5: (mine, far_down), 6: (mine, far_up), 7: (mine, far_far),
    }

    def ag_start(s, j):
        ag_copy(s, j, *sends[j]).start()

    def ag_wait(s, j):
        ag_copy(s, j, *arrivals[j], across).wait_recv()

    def as_copy(s, source, of):
        block = p_all.at[s, pl.ds(of * chips, chips), source]
        return remote(block, block, as_ss.at[s, source], as_rs.at[s, source], sibling)

    def pack(s):
        b_copy(s, 1 - core).wait_recv()
        for t in range(chips):
            k = core * chips + t
            block = p_recv[s][by_k[5, s, chip * n_cols + k], by_k[1, s, chip * n_cols + k]]
            valid = by_k[0, s, chip * n_cols + k] == 1
            p_all[s, k, me_r] = jnp.where(valid, block, jnp.zeros_like(block))

    def ag_first(s):
        for j in (0, 1, 2):
            ag_start(s, j)
        as_copy(s, me_r, core).start()

    def ag_second(s):
        ag_wait(s, 2)
        ag_start(s, 5)
        ag_start(s, 6)
        ag_wait(s, 0)
        ag_start(s, 3)
        ag_wait(s, 1)
        ag_start(s, 4)
        for source in (across, down, up):
            as_copy(s, source, core).start()

    def ag_third(s):
        ag_wait(s, 3)
        ag_wait(s, 4)
        ag_start(s, 7)
        ag_wait(s, 5)
        ag_wait(s, 6)
        for source in (far, far_down, far_up):
            as_copy(s, source, core).start()
        ag_wait(s, 7)
        as_copy(s, far_far, core).start()

    def l_copy(t):
        k = core * chips + t
        return remote(p_all.at[:, k, me_r], l_recv.at[chip], l_ss.at[t], l_rs.at[chip], (me_r, k))

    def l_arrive(j):
        return remote(p_all.at[:, 0, me_r], l_recv.at[j], l_ss.at[0], l_rs.at[j], sibling)

    def l_first():
        @pl.loop(0, chips)
        def _(t):
            k = core * chips + t

            @pl.when(k != me_c)
            def _():
                l_copy(t).start()

            @pl.when(k == me_c)
            def _():
                l_recv[chip] = p_all[:, k, me_r]

    def m_copy(d):
        g = lax.rem(me_r + d, n_rows)
        return remote(l_recv.at[g], left.at[:, me_r], m_ss.at[d], m_rs.at[d], (g, me_c))

    def m_arrive(d):
        source = lax.rem(me_r - d + n_rows, n_rows)
        return remote(l_recv.at[0], left.at[:, source], m_ss.at[d], m_rs.at[d], (source, me_c))

    def l_second():
        @pl.loop(0, chips)
        def _(j):
            @pl.when(2 * j + me_c // chips != me_c)
            def _():
                l_arrive(j).wait_recv()

        left[:, me_r] = l_recv[me_r]

        @pl.loop(1, n_rows)
        def _(d):
            m_copy(d).start()

    to_cores(0)
    pack(0)
    ag_first(0)
    picks(1)
    to_cores(1)
    ag_second(0)
    pack(1)
    ag_first(1)
    l_first()
    ag_third(0)
    ag_second(1)

    def c_copy(s, h):
        return remote(part.at[s, 0, h], core_recv.at[s, h], c_ss.at[s, h], c_rs.at[s, h], sibling)

    def z_copy(s, h, d):
        to = (me_r, (x_hi * zs + lax.rem(z + d, zs)) * 2 + core)
        return remote(z_send.at[s, h, d - 1], z_recv.at[s, h, d - 1], z_ss.at[s, h, d], z_rs.at[s, h, d], to)

    def products(s):
        @pl.loop(0, n_rows)
        def _(source):
            as_copy(s, source, 1 - core).wait_recv()

        def product(half_of, h):
            rows = pl.ds(pl.multiple_of((half_of * chips + h * zs) * BS, BS), zs * BS)
            result = jnp.dot(a_pick[s, rows, :], p_all[s].reshape(n_cols * BS, width), preferred_element_type=F32)
            part[s, half_of, h] = result.reshape(zs, BS, width)

        def to_z(h):
            c_copy(s, h).wait_recv()

            @pl.loop(1, zs)
            def _(d):
                there = lax.rem(z + d, zs)
                encode(z_send.at[s, h, d - 1], part[s, 1, h, there] + core_recv[s, h, there])
                z_copy(s, h, d).start()

        @pl.loop(0, x_his)
        def _(step):
            h = jnp.where(step == 0, 1 - x_hi, x_hi)
            product(0, h)
            c_copy(s, h).start()

            @pl.when(step > 0)
            def _():
                to_z(1 - x_hi)

            product(1, h)

        to_z(x_hi)

    products(0)
    ag_third(1)
    l_second()
    products(1)

    @pl.loop(1, n_rows)
    def _(d):
        m_arrive(d).wait_recv()

    def x_copy(s):
        to = (me_r, ((1 - x_hi) * zs + z) * 2 + core)
        return remote(x_send.at[s], x_recv.at[s], x_ss.at[s], x_rs.at[s], to)

    def over_z(s, h):
        total = part[s, 1, h, z] + core_recv[s, h, z]
        for d in range(1, zs):
            z_copy(s, h, d).wait_recv()
            total = total + decode(z_recv.at[s, h, d - 1])
        return total

    def start_x(s):
        encode(x_send.at[s], over_z(s, 1 - x_hi))
        x_copy(s).start()

    half = width // 2
    ring = zs
    piece, bit = half // ring, half // ring // ring
    x_at = x_hi * 2 + x_lo

    def ds_copy(s):
        there = pl.ds(pl.multiple_of((1 - core) * half, half), half)
        return remote(d_part.at[s, there], d_sib.at[s], ds_ss.at[s], ds_rs.at[s], sibling)

    def place_in(f, step):
        return y if f == step else z

    def peer_at(f, step, d):
        if step == 2:
            peer = lax.rem(x_at + d, ring)
            return peer, (lax.rem(peer, 2) * ys + y, ((peer // 2) * zs + z) * 2 + core)
        peer = lax.rem(place_in(f, step) + d, ring)
        return peer, (x_lo * ys + peer, me_c) if f == step else (me_r, (x_hi * zs + peer) * 2 + core)

    def u_copy(s, f, d):
        peer, to = peer_at(f, 0, d)
        return remote(u_send.at[s, f, peer], u_recv.at[s, f, d], u_ss.at[s, f, d], u_rs.at[s, f, d], to)

    def v_copy(s, f, d):
        peer, to = peer_at(f, 1, d)
        return remote(v_send.at[s, f, peer], v_recv.at[s, f, d], v_ss.at[s, f, d], v_rs.at[s, f, d], to)

    def t_copy(s, f, d, source):
        block = t_all.at[s, f, source]
        return remote(block, block, t_ss.at[s, f, d], t_rs.at[s, f, d], peer_at(f, 2, d)[1])

    def block_of(s, f, first, rows):
        return diag.at[s, pl.ds(pl.multiple_of(first, rows), rows), f * half : (f + 1) * half]

    def w_copy(s, f, d, source):
        block = block_of(s, f, core * half + place_in(f, 0) * piece + source * bit, bit)
        return remote(block, block, w_ss.at[s, f, d], w_rs.at[s, f, d], peer_at(f, 1, d)[1])

    def er_copy(s, f, d, source):
        block = block_of(s, f, core * half + source * piece, piece)
        return remote(block, block, er_ss.at[s, f, d], er_rs.at[s, f, d], peer_at(f, 0, d)[1])

    def es_copy(s, f, of):
        block = block_of(s, f, of * half, half)
        return remote(block, block, es_ss.at[s, f], es_rs.at[s, f], sibling)

    def finish_sums(s):
        total = over_z(s, x_hi)
        x_copy(s).wait_recv()
        total = total + decode(x_recv.at[s])
        valid = by_k[0, s, me_r * n_cols + me_c] == 1
        total = jnp.where(valid, total, jnp.zeros_like(total))
        out[s] = total
        total = -total
        high = total.astype(BF16)
        low = (total - high.astype(F32)).astype(BF16)
        contract = functools.partial(
            lax.dot_general, dimension_numbers=(((0,), (0,)), ((), ())), preferred_element_type=F32
        )
        for of in (1 - core, core):
            columns = pl.ds(pl.multiple_of(of * half, half), half)
            block = left[s, :, :, columns].reshape(BS, half)
            d_part[s, columns] = contract(block, high) + contract(block, low)
            if of is not core:
                ds_copy(s).start()

    def over_cores(s):
        ds_copy(s).wait_recv()
        here = pl.ds(pl.multiple_of(core * half, half), half)
        total = (d_part[s, here] + d_sib[s]).reshape(ring, piece, width)
        for f in range(2):
            u_send[s, f] = total[:, :, f * half : (f + 1) * half]
            for d in range(1, ring):
                u_copy(s, f, d).start()

    def over_first(s):
        for f in range(2):
            total = u_send[s, f, place_in(f, 0)]
            for d in range(1, ring):
                u_copy(s, f, d).wait_recv()
                total = total + u_recv[s, f, d]
            v_send[s, f] = total.reshape(ring, bit, half)
            for d in range(1, ring):
                v_copy(s, f, d).start()

    def over_second(s):
        for f in range(2):
            total = v_send[s, f, place_in(f, 1)]
            for d in range(1, ring):
                v_copy(s, f, d).wait_recv()
                total = total + v_recv[s, f, d]
            t_all[s, f, x_at] = total
            for d in range(1, ring):
                t_copy(s, f, d, x_at).start()

    def over_third(s):
        for f in range(2):
            for d in range(1, ring):
                t_copy(s, f, d, lax.rem(x_at - d + ring, ring)).wait_recv()
            total = t_all[s, f, 0]
            for x in range(1, ring):
                total = total + t_all[s, f, x]
            first = core * half + place_in(f, 0) * piece + place_in(f, 1) * bit
            diag[s, pl.ds(pl.multiple_of(first, bit), bit), f * half : (f + 1) * half] = total
            for d in range(1, ring):
                w_copy(s, f, d, place_in(f, 1)).start()

    def back_second(s):
        for f in range(2):
            for d in range(1, ring):
                w_copy(s, f, d, lax.rem(place_in(f, 1) - d + ring, ring)).wait_recv()
            for d in range(1, ring):
                er_copy(s, f, d, place_in(f, 0)).start()

    def back_first(s):
        for f in range(2):
            for d in range(1, ring):
                er_copy(s, f, d, lax.rem(place_in(f, 0) - d + ring, ring)).wait_recv()
            es_copy(s, f, core).start()

    start_x(0)
    finish_sums(0)
    over_cores(0)
    start_x(1)
    over_first(0)
    finish_sums(1)
    over_second(0)
    over_cores(1)
    over_third(0)
    over_first(1)
    back_second(0)
    over_second(1)
    back_first(0)
    over_third(1)
    back_second(1)
    back_first(1)

    for s in range(supers):
        @pl.loop(1, n_cols)
        def _(d, s=s):
            p_copy(s, d, me_c).wait_send()

        b_copy(s, core).wait_send()

    @pl.loop(0, chips)
    def _(t):
        @pl.when(core * chips + t != me_c)
        def _():
            l_copy(t).wait_send()

    @pl.loop(1, n_rows)
    def _(d):
        m_copy(d).wait_send()

    for s in range(supers):
        for j in sends:
            ag_copy(s, j, *sends[j]).wait_send()

        @pl.loop(0, n_rows)
        def _(source, s=s):
            as_copy(s, source, core).wait_send()

        for f in range(2):
            for d in range(1, ring):
                u_copy(s, f, d).wait_send()
                v_copy(s, f, d).wait_send()
                t_copy(s, f, d, x_at).wait_send()
                w_copy(s, f, d, place_in(f, 1)).wait_send()
                er_copy(s, f, d, place_in(f, 0)).wait_send()

            es_copy(s, f, core).wait_send()
            es_copy(s, f, 1 - core).wait_recv()

        for h in range(x_his):
            c_copy(s, h).wait_send()
            for d in range(1, zs):
                z_copy(s, h, d).wait_send()
        x_copy(s).wait_send()
        ds_copy(s).wait_send()


def local(n_rows, n_cols, inverse, panels, block_slot, list_ids):
    supers, _, width = panels.shape
    col_blocks = inverse.shape[1] // BS
    sub = BS // n_rows
    x_his = 2
    chips = n_cols // 2
    zs = chips // x_his
    half = width // 2
    lists = tables(block_slot, list_ids, n_rows, n_cols)
    blocks = inverse.reshape(-1, BS, inverse.shape[1])
    slices = panels.reshape(supers, -1, n_rows, sub, width)
    vmem = pl.BlockSpec(memory_space=pltpu.VMEM)
    smem = pl.BlockSpec(memory_space=pltpu.SMEM)
    dma = pltpu.SemaphoreType.DMA
    scratch = [
        pltpu.VMEM((supers, slices.shape[1], sub, width), BF16),
        pltpu.VMEM((col_blocks, blocks.shape[0], BS, BS), BF16),
        pltpu.VMEM((supers, n_cols * BS, n_cols * BS), BF16),
        pltpu.VMEM((supers, n_cols, sub, width), BF16),
        pltpu.VMEM((2, n_cols, sub, width), BF16),
        pltpu.VMEM((2, n_cols, sub, width), BF16),
        pltpu.VMEM((supers, n_cols, n_rows, sub, width), BF16),
        pltpu.VMEM((chips, supers, sub, width), BF16),
        pltpu.VMEM((supers, n_rows, sub, width), BF16),
        pltpu.VMEM((supers, 2, x_his, zs, BS, width), F32),
        pltpu.VMEM((supers, x_his, zs, BS, width), F32),
        pltpu.VMEM((supers, x_his, zs - 1, BS + SCALE_ROWS, width), jnp.int16),
        pltpu.VMEM((supers, x_his, zs - 1, BS + SCALE_ROWS, width), jnp.int16),
        pltpu.VMEM((supers, BS + SCALE_ROWS, width), jnp.int16),
        pltpu.VMEM((supers, BS + SCALE_ROWS, width), jnp.int16),
        pltpu.VMEM((supers, width, width), F32),
        pltpu.VMEM((supers, half, width), F32),
        pltpu.VMEM((supers, 2, zs, half // zs, half), F32),
        pltpu.VMEM((supers, 2, zs, half // zs, half), F32),
        pltpu.VMEM((supers, 2, zs, half // zs // zs, half), F32),
        pltpu.VMEM((supers, 2, zs, half // zs // zs, half), F32),
        pltpu.VMEM((supers, 2, zs, half // zs // zs, half), F32),
        dma(()),
        dma((col_blocks,)),
        dma((supers, n_cols)), dma((supers, n_cols)),
        dma((supers,)), dma((supers,)),
        dma((supers, 8)), dma((supers, 8)),
        dma((supers, n_rows)), dma((supers, n_rows)),
        dma((chips,)), dma((chips,)),
        dma((n_rows,)), dma((n_rows,)),
        dma((supers, x_his)), dma((supers, x_his)),
        dma((supers, x_his, zs)), dma((supers, x_his, zs)),
        dma((supers,)), dma((supers,)),
        dma((supers,)), dma((supers,)),
        dma((supers, 2, zs)), dma((supers, 2, zs)),
        dma((supers, 2, zs)), dma((supers, 2, zs)),
        dma((supers, 2, zs)), dma((supers, 2, zs)),
        dma((supers, 2, zs)), dma((supers, 2, zs)),
        dma((supers, 2, zs)), dma((supers, 2, zs)),
        dma((supers, 2)), dma((supers, 2)),
    ]
    return pl.pallas_call(
        functools.partial(kernel, n_rows, n_cols, x_his),
        out_shape=(
            pltpu.VMEM((supers, BS, width), F32),
            pltpu.VMEM((supers, width, width), F32),
        ),
        in_specs=[pl.BlockSpec(memory_space=pl.ANY), pl.BlockSpec(memory_space=pl.ANY), smem, smem],
        out_specs=(vmem, vmem),
        scratch_shapes=scratch,
        compiler_params=pltpu.CompilerParams(
            collective_id=0, has_side_effects=True, vmem_limit_bytes=60 * 2**20
        ),
    )(blocks, slices, *lists)


def solution(mesh):
    n_rows, n_cols = mesh.shape["row"], mesh.shape["col"]
    return jax.shard_map(
        functools.partial(local, n_rows, n_cols),
        mesh=mesh,
        in_specs=(P("row", "col"), P(None, "col", None), P(), P()),
        out_specs=(P(None, ("row", "col"), None), P()),
        check_vma=False,
    )
```

```python
import functools

import jax
import jax.numpy as jnp
from jax import lax
from jax.experimental import pallas as pl
from jax.experimental.pallas import tpu as pltpu
from jax.sharding import PartitionSpec as P

BS = 128
MESH = pl.DeviceIdType.MESH
F32 = jnp.float32
BF16 = jnp.bfloat16


def tables(block_slot, list_ids, n_rows, n_cols):
    n_blocks, listed = block_slot.shape[0], list_ids.shape[1]
    ids = jnp.arange(n_blocks, dtype=jnp.int32)
    slots = jnp.sum(jnp.where(list_ids[..., None] == ids, block_slot, 0), axis=-1)
    col_blocks, row_blocks = n_blocks // n_cols, n_blocks // n_rows
    row = slots // row_blocks
    pos = jnp.arange(listed, dtype=jnp.int32)
    before = pos[None, :] < pos[:, None]
    kth = jnp.sum(((row[:, :, None] == row[:, None, :]) & before).astype(jnp.int32), axis=-1)
    key = row * n_cols + kth
    keys = jnp.arange(n_rows * n_cols, dtype=jnp.int32)
    code = jnp.sum(jnp.where(key[:, None, :] == keys[:, None], (1 + slots * listed + pos)[:, None, :], 0), axis=-1)
    slot, place = jnp.maximum(code - 1, 0) // listed, jnp.maximum(code - 1, 0) % listed
    shard = listed // n_cols
    table = jnp.stack(
        [
            (code > 0).astype(jnp.int32), place // shard, slot // col_blocks, slot % col_blocks, slot % row_blocks,
            slot // col_blocks % 2,
        ]
    )
    return slots // col_blocks, table


SCALE_ROWS = 16
TOP = 32000.0


def encode(ref, block):
    top = jnp.max(jnp.abs(block), axis=0, keepdims=True)
    exponent = jnp.floor(jnp.log2(jnp.maximum(top, 1e-30))) + 1.0
    coded = jnp.round(block * (jnp.exp2(-exponent) * TOP))
    ref[0:BS] = coded.astype(jnp.int32).astype(jnp.int16)
    exponents = jnp.broadcast_to(exponent, (SCALE_ROWS, block.shape[1]))
    ref[BS : BS + SCALE_ROWS] = exponents.astype(jnp.int32).astype(jnp.int16)


def decode(ref):
    exponent = ref[BS : BS + SCALE_ROWS].astype(jnp.int32).astype(F32)[0:1]
    return ref[0:BS].astype(jnp.int32).astype(F32) * (jnp.exp2(exponent) * (1.0 / TOP))


def kernel(
    n_rows, n_cols, x_his,
    inv_hbm, pan_hbm, cols, by_k,
    out, diag,
    pan, a_all, a_pick, p_send, p_recv_0, p_recv_1, p_all, l_recv, left,
    part, core_recv, z_send, z_recv, x_send, x_recv, d_part, d_sib, u_send, u_recv, v_send, v_recv, t_all,
    pan_sem, a_sem, p_ss, p_rs, b_ss, b_rs, ag_ss, ag_rs, as_ss, as_rs, l_ss, l_rs, m_ss, m_rs, c_ss, c_rs, z_ss, z_rs, x_ss, x_rs,
    ds_ss, ds_rs, u_ss, u_rs, v_ss, v_rs, t_ss, t_rs, w_ss, w_rs, er_ss, er_rs, es_ss, es_rs,
):
    supers = pan.shape[0]
    p_recv = (p_recv_0, p_recv_1)
    sub = BS // n_rows
    col_blocks = a_all.shape[0]
    shard = pan.shape[1]
    width = pan.shape[3]
    chips = n_cols // 2
    zs = chips // x_his
    ys = n_rows // 2
    me_r, me_c = lax.axis_index("row"), lax.axis_index("col")
    core = lax.rem(me_c, 2)
    chip = me_c // 2
    x_hi, z = chip // zs, lax.rem(chip, zs)
    sibling = (me_r, me_c + 1 - 2 * core)

    def remote(src, dst, ss, rs, to):
        return pltpu.make_async_remote_copy(
            src_ref=src, dst_ref=dst, send_sem=ss, recv_sem=rs, device_id=to, device_id_type=MESH
        )

    barrier = pltpu.get_barrier_semaphore()

    @pl.loop(1, n_cols)
    def _(d):
        pl.semaphore_signal(barrier, inc=1, device_id=(me_r, lax.rem(me_c + d, n_cols)), device_id_type=MESH)

    @pl.loop(1, n_rows)
    def _(d):
        pl.semaphore_signal(barrier, inc=1, device_id=(lax.rem(me_r + d, n_rows), me_c), device_id_type=MESH)

    opposite = (lax.rem(me_r + ys, n_rows), lax.rem(me_c + zs * 2, n_cols))
    pl.semaphore_signal(barrier, inc=1, device_id=opposite, device_id_type=MESH)

    load_pan = pltpu.make_async_copy(pan_hbm.at[:, :, me_r], pan, pan_sem)
    load_pan.start()

    def load_a(b):
        columns = pl.ds(pl.multiple_of(b * BS, BS), BS)
        return pltpu.make_async_copy(inv_hbm.at[:, :, columns], a_all.at[b], a_sem.at[b])

    @pl.loop(0, col_blocks)
    def _(b):
        load_a(b).start()

    load_pan.wait()

    def pick_for(c, s):
        piece = jnp.zeros((sub, width), BF16)
        for q in range(shard):
            piece = jnp.where(cols[s, me_c * shard + q] == c, pan[s, q], piece)
        return piece

    @pl.loop(1, n_cols)
    def _(d):
        for s in range(supers):
            p_send[s, d] = pick_for(lax.rem(me_c + d, n_cols), s)

    for s in range(supers):
        p_recv[s][core, me_c] = pick_for(me_c, s)

    pl.semaphore_wait(barrier, n_cols + n_rows - 1)

    def p_copy(s, d, source):
        to = (me_r, lax.rem(me_c + d, n_cols))
        return remote(p_send.at[s, d], p_recv[s].at[lax.rem(to[1], 2), source], p_ss.at[s, d], p_rs.at[s, d], to)

    for s in range(supers):
        @pl.loop(1, n_cols)
        def _(d, s=s):
            p_copy(s, d, me_c).start()

    def picks(s):
        @pl.loop(0, n_cols)
        def _(i):
            half_of, place = i // chips, lax.rem(i, chips)
            k = 2 * place + jnp.where(half_of == 1, core, 1 - core)
            a_row = by_k[4, s, me_r * n_cols + k]
            rows = pl.ds(pl.multiple_of(i * BS, BS), BS)
            for b in range(n_cols):
                block = a_all[by_k[3, s, chip * n_cols + b], a_row]
                here = by_k[0, s, chip * n_cols + b] * (by_k[2, s, chip * n_cols + b] == me_c) == 1
                a_pick[s, rows, b * BS : (b + 1) * BS] = jnp.where(here, block, jnp.zeros_like(block))

    @pl.loop(0, col_blocks)
    def _(b):
        load_a(b).wait()

    picks(0)

    def b_copy(s, of):
        return remote(p_recv[s].at[of], p_recv[s].at[of], b_ss.at[s], b_rs.at[s], sibling)

    def to_cores(s):
        @pl.loop(1, n_cols)
        def _(d):
            source = lax.rem(me_c - d + n_cols, n_cols)
            remote(p_send.at[s, d], p_recv[s].at[core, source], p_ss.at[s, d], p_rs.at[s, d], sibling).wait_recv()

        b_copy(s, core).start()

    mine = pl.ds(core * chips, chips)
    x_lo, y = me_r // ys, lax.rem(me_r, ys)
    up, down, across = x_lo * ys + lax.rem(y + 1, ys), x_lo * ys + lax.rem(y + ys - 1, ys), (1 - x_lo) * ys + y
    far = x_lo * ys + lax.rem(y + 2, ys)
    far_up, far_down = lax.rem(up + ys, n_rows), lax.rem(down + ys, n_rows)
    far_far = lax.rem(far + ys, n_rows)

    def ag_copy(s, j, source, to):
        block = p_all.at[s, mine, source]
        return remote(block, block, ag_ss.at[s, j], ag_rs.at[s, j], (to, me_c))

    sends = {
        0: (me_r, up), 1: (me_r, down), 2: (me_r, across), 3: (me_r, far),
        4: (across, up), 5: (across, down), 6: (far, across),
    }
    arrivals = {
        0: down, 1: up, 2: across, 3: far, 4: far_down, 5: far_up, 6: far_far,
    }

    def ag_start(s, j):
        ag_copy(s, j, *sends[j]).start()

    def ag_wait(s, j):
        ag_copy(s, j, arrivals[j], across).wait_recv()

    def as_copy(s, source, of):
        block = p_all.at[s, pl.ds(of * chips, chips), source]
        return remote(block, block, as_ss.at[s, source], as_rs.at[s, source], sibling)

    def pack(s):
        b_copy(s, 1 - core).wait_recv()
        for t in range(chips):
            k = core * chips + t
            block = p_recv[s][by_k[5, s, chip * n_cols + k], by_k[1, s, chip * n_cols + k]]
            valid = by_k[0, s, chip * n_cols + k] == 1
            p_all[s, k, me_r] = jnp.where(valid, block, jnp.zeros_like(block))

    def ag_first(s):
        for j in (2, 0, 1, 3):
            ag_start(s, j)
        as_copy(s, me_r, core).start()

    def ag_second(s):
        ag_wait(s, 2)
        ag_start(s, 4)
        ag_start(s, 5)
        ag_wait(s, 0)
        ag_wait(s, 1)
        for source in (across, down, up):
            as_copy(s, source, core).start()

    def ag_third(s):
        ag_wait(s, 3)
        ag_start(s, 6)
        as_copy(s, far, core).start()
        for j, source in ((4, far_down), (5, far_up), (6, far_far)):
            ag_wait(s, j)
            as_copy(s, source, core).start()

    def l_copy(t):
        k = core * chips + t
        return remote(p_all.at[:, k, me_r], l_recv.at[chip], l_ss.at[t], l_rs.at[chip], (me_r, k))

    def l_arrive(j):
        return remote(p_all.at[:, 0, me_r], l_recv.at[j], l_ss.at[0], l_rs.at[j], sibling)

    def l_first():
        @pl.loop(0, chips)
        def _(t):
            k = core * chips + t

            @pl.when(k != me_c)
            def _():
                l_copy(t).start()

            @pl.when(k == me_c)
            def _():
                l_recv[chip] = p_all[:, k, me_r]

    def m_copy(d):
        g = lax.rem(me_r + d, n_rows)
        return remote(l_recv.at[g], left.at[:, me_r], m_ss.at[d], m_rs.at[d], (g, me_c))

    def m_arrive(d):
        source = lax.rem(me_r - d + n_rows, n_rows)
        return remote(l_recv.at[0], left.at[:, source], m_ss.at[d], m_rs.at[d], (source, me_c))

    def l_second():
        @pl.loop(0, chips)
        def _(j):
            @pl.when(2 * j + me_c // chips != me_c)
            def _():
                l_arrive(j).wait_recv()

        left[:, me_r] = l_recv[me_r]

        @pl.loop(1, n_rows)
        def _(d):
            m_copy(d).start()

    to_cores(0)
    pack(0)
    ag_first(0)
    picks(1)
    to_cores(1)
    ag_second(0)
    pack(1)
    ag_first(1)
    l_first()
    ag_third(0)
    ag_second(1)

    def c_copy(s, h):
        return remote(part.at[s, 0, h], core_recv.at[s, h], c_ss.at[s, h], c_rs.at[s, h], sibling)

    def z_copy(s, h, d):
        to = (me_r, (x_hi * zs + lax.rem(z + d, zs)) * 2 + core)
        return remote(z_send.at[s, h, d - 1], z_recv.at[s, h, d - 1], z_ss.at[s, h, d], z_rs.at[s, h, d], to)

    def products(s):
        @pl.loop(0, n_rows)
        def _(source):
            as_copy(s, source, 1 - core).wait_recv()

        def product(half_of, h):
            rows = pl.ds(pl.multiple_of((half_of * chips + h * zs) * BS, BS), zs * BS)
            result = jnp.dot(a_pick[s, rows, :], p_all[s].reshape(n_cols * BS, width), preferred_element_type=F32)
            part[s, half_of, h] = result.reshape(zs, BS, width)

        def to_z(h):
            c_copy(s, h).wait_recv()

            @pl.loop(1, zs)
            def _(d):
                there = lax.rem(z + d, zs)
                encode(z_send.at[s, h, d - 1], part[s, 1, h, there] + core_recv[s, h, there])
                z_copy(s, h, d).start()

        @pl.loop(0, x_his)
        def _(step):
            h = jnp.where(step == 0, 1 - x_hi, x_hi)
            product(0, h)
            c_copy(s, h).start()

            @pl.when(step > 0)
            def _():
                to_z(1 - x_hi)

            product(1, h)

        to_z(x_hi)

    products(0)
    ag_third(1)
    l_second()
    products(1)

    @pl.loop(1, n_rows)
    def _(d):
        m_arrive(d).wait_recv()

    def x_copy(s):
        to = (me_r, ((1 - x_hi) * zs + z) * 2 + core)
        return remote(x_send.at[s], x_recv.at[s], x_ss.at[s], x_rs.at[s], to)

    def over_z(s, h):
        total = part[s, 1, h, z] + core_recv[s, h, z]
        for d in range(1, zs):
            z_copy(s, h, d).wait_recv()
            total = total + decode(z_recv.at[s, h, d - 1])
        return total

    def start_x(s):
        encode(x_send.at[s], over_z(s, 1 - x_hi))
        x_copy(s).start()

    half = width // 2
    ring = zs
    piece, bit = half // ring, half // ring // ring
    x_at = x_hi * 2 + x_lo

    def ds_copy(s):
        there = pl.ds(pl.multiple_of((1 - core) * half, half), half)
        return remote(d_part.at[s, there], d_sib.at[s], ds_ss.at[s], ds_rs.at[s], sibling)

    def place_in(f, step):
        return y if f == step else z

    def peer_at(f, step, d):
        if step == 2:
            peer = lax.rem(x_at + d, ring)
            return peer, (lax.rem(peer, 2) * ys + y, ((peer // 2) * zs + z) * 2 + core)
        peer = lax.rem(place_in(f, step) + d, ring)
        return peer, (x_lo * ys + peer, me_c) if f == step else (me_r, (x_hi * zs + peer) * 2 + core)

    def u_copy(s, f, d):
        peer, to = peer_at(f, 0, d)
        return remote(u_send.at[s, f, peer], u_recv.at[s, f, d], u_ss.at[s, f, d], u_rs.at[s, f, d], to)

    def v_copy(s, f, d):
        peer, to = peer_at(f, 1, d)
        return remote(v_send.at[s, f, peer], v_recv.at[s, f, d], v_ss.at[s, f, d], v_rs.at[s, f, d], to)

    def t_copy(s, f, d, source):
        block = t_all.at[s, f, source]
        return remote(block, block, t_ss.at[s, f, d], t_rs.at[s, f, d], peer_at(f, 2, d)[1])

    def block_of(s, f, first, rows):
        return diag.at[s, pl.ds(pl.multiple_of(first, rows), rows), f * half : (f + 1) * half]

    def w_copy(s, f, d, source):
        block = block_of(s, f, core * half + place_in(f, 0) * piece + source * bit, bit)
        return remote(block, block, w_ss.at[s, f, d], w_rs.at[s, f, d], peer_at(f, 1, d)[1])

    def er_copy(s, f, d, source):
        block = block_of(s, f, core * half + source * piece, piece)
        return remote(block, block, er_ss.at[s, f, d], er_rs.at[s, f, d], peer_at(f, 0, d)[1])

    def es_copy(s, f, of):
        block = block_of(s, f, of * half, half)
        return remote(block, block, es_ss.at[s, f], es_rs.at[s, f], sibling)

    def finish_sums(s):
        total = over_z(s, x_hi)
        x_copy(s).wait_recv()
        total = total + decode(x_recv.at[s])
        valid = by_k[0, s, me_r * n_cols + me_c] == 1
        total = jnp.where(valid, total, jnp.zeros_like(total))
        out[s] = total
        total = -total
        high = total.astype(BF16)
        low = (total - high.astype(F32)).astype(BF16)
        contract = functools.partial(
            lax.dot_general, dimension_numbers=(((0,), (0,)), ((), ())), preferred_element_type=F32
        )
        for of in (1 - core, core):
            columns = pl.ds(pl.multiple_of(of * half, half), half)
            block = left[s, :, :, columns].reshape(BS, half)
            d_part[s, columns] = contract(block, high) + contract(block, low)
            if of is not core:
                ds_copy(s).start()

    def over_cores(s):
        ds_copy(s).wait_recv()
        here = pl.ds(pl.multiple_of(core * half, half), half)
        total = (d_part[s, here] + d_sib[s]).reshape(ring, piece, width)
        for f in range(2):
            u_send[s, f] = total[:, :, f * half : (f + 1) * half]
            for d in range(1, ring):
                u_copy(s, f, d).start()

    def over_first(s):
        for f in range(2):
            total = u_send[s, f, place_in(f, 0)]
            for d in range(1, ring):
                u_copy(s, f, d).wait_recv()
                total = total + u_recv[s, f, d]
            v_send[s, f] = total.reshape(ring, bit, half)
            for d in range(1, ring):
                v_copy(s, f, d).start()

    def over_second(s):
        for f in range(2):
            total = v_send[s, f, place_in(f, 1)]
            for d in range(1, ring):
                v_copy(s, f, d).wait_recv()
                total = total + v_recv[s, f, d]
            t_all[s, f, x_at] = total
            for d in range(1, ring):
                t_copy(s, f, d, x_at).start()

    def over_third(s):
        for f in range(2):
            for d in range(1, ring):
                t_copy(s, f, d, lax.rem(x_at - d + ring, ring)).wait_recv()
            total = t_all[s, f, 0]
            for x in range(1, ring):
                total = total + t_all[s, f, x]
            first = core * half + place_in(f, 0) * piece + place_in(f, 1) * bit
            diag[s, pl.ds(pl.multiple_of(first, bit), bit), f * half : (f + 1) * half] = total
            for d in range(1, ring):
                w_copy(s, f, d, place_in(f, 1)).start()

    def back_second(s):
        for f in range(2):
            for d in range(1, ring):
                w_copy(s, f, d, lax.rem(place_in(f, 1) - d + ring, ring)).wait_recv()
            for d in range(1, ring):
                er_copy(s, f, d, place_in(f, 0)).start()

    def back_first(s):
        for f in range(2):
            for d in range(1, ring):
                er_copy(s, f, d, lax.rem(place_in(f, 0) - d + ring, ring)).wait_recv()
            es_copy(s, f, core).start()

    start_x(0)
    finish_sums(0)
    over_cores(0)
    start_x(1)
    over_first(0)
    finish_sums(1)
    over_second(0)
    over_cores(1)
    over_third(0)
    over_first(1)
    back_second(0)
    over_second(1)
    back_first(0)
    over_third(1)
    back_second(1)
    back_first(1)

    for s in range(supers):
        @pl.loop(1, n_cols)
        def _(d, s=s):
            p_copy(s, d, me_c).wait_send()

        b_copy(s, core).wait_send()

    @pl.loop(0, chips)
    def _(t):
        @pl.when(core * chips + t != me_c)
        def _():
            l_copy(t).wait_send()

    @pl.loop(1, n_rows)
    def _(d):
        m_copy(d).wait_send()

    for s in range(supers):
        for j in sends:
            ag_copy(s, j, *sends[j]).wait_send()

        @pl.loop(0, n_rows)
        def _(source, s=s):
            as_copy(s, source, core).wait_send()

        for f in range(2):
            for d in range(1, ring):
                u_copy(s, f, d).wait_send()
                v_copy(s, f, d).wait_send()
                t_copy(s, f, d, x_at).wait_send()
                w_copy(s, f, d, place_in(f, 1)).wait_send()
                er_copy(s, f, d, place_in(f, 0)).wait_send()

            es_copy(s, f, core).wait_send()
            es_copy(s, f, 1 - core).wait_recv()

        for h in range(x_his):
            c_copy(s, h).wait_send()
            for d in range(1, zs):
                z_copy(s, h, d).wait_send()
        x_copy(s).wait_send()
        ds_copy(s).wait_send()


def local(n_rows, n_cols, inverse, panels, block_slot, list_ids):
    supers, _, width = panels.shape
    col_blocks = inverse.shape[1] // BS
    sub = BS // n_rows
    x_his = 2
    chips = n_cols // 2
    zs = chips // x_his
    half = width // 2
    lists = tables(block_slot, list_ids, n_rows, n_cols)
    blocks = inverse.reshape(-1, BS, inverse.shape[1])
    slices = panels.reshape(supers, -1, n_rows, sub, width)
    vmem = pl.BlockSpec(memory_space=pltpu.VMEM)
    smem = pl.BlockSpec(memory_space=pltpu.SMEM)
    dma = pltpu.SemaphoreType.DMA
    scratch = [
        pltpu.VMEM((supers, slices.shape[1], sub, width), BF16),
        pltpu.VMEM((col_blocks, blocks.shape[0], BS, BS), BF16),
        pltpu.VMEM((supers, n_cols * BS, n_cols * BS), BF16),
        pltpu.VMEM((supers, n_cols, sub, width), BF16),
        pltpu.VMEM((2, n_cols, sub, width), BF16),
        pltpu.VMEM((2, n_cols, sub, width), BF16),
        pltpu.VMEM((supers, n_cols, n_rows, sub, width), BF16),
        pltpu.VMEM((chips, supers, sub, width), BF16),
        pltpu.VMEM((supers, n_rows, sub, width), BF16),
        pltpu.VMEM((supers, 2, x_his, zs, BS, width), F32),
        pltpu.VMEM((supers, x_his, zs, BS, width), F32),
        pltpu.VMEM((supers, x_his, zs - 1, BS + SCALE_ROWS, width), jnp.int16),
        pltpu.VMEM((supers, x_his, zs - 1, BS + SCALE_ROWS, width), jnp.int16),
        pltpu.VMEM((supers, BS + SCALE_ROWS, width), jnp.int16),
        pltpu.VMEM((supers, BS + SCALE_ROWS, width), jnp.int16),
        pltpu.VMEM((supers, width, width), F32),
        pltpu.VMEM((supers, half, width), F32),
        pltpu.VMEM((supers, 2, zs, half // zs, half), F32),
        pltpu.VMEM((supers, 2, zs, half // zs, half), F32),
        pltpu.VMEM((supers, 2, zs, half // zs // zs, half), F32),
        pltpu.VMEM((supers, 2, zs, half // zs // zs, half), F32),
        pltpu.VMEM((supers, 2, zs, half // zs // zs, half), F32),
        dma(()),
        dma((col_blocks,)),
        dma((supers, n_cols)), dma((supers, n_cols)),
        dma((supers,)), dma((supers,)),
        dma((supers, 8)), dma((supers, 8)),
        dma((supers, n_rows)), dma((supers, n_rows)),
        dma((chips,)), dma((chips,)),
        dma((n_rows,)), dma((n_rows,)),
        dma((supers, x_his)), dma((supers, x_his)),
        dma((supers, x_his, zs)), dma((supers, x_his, zs)),
        dma((supers,)), dma((supers,)),
        dma((supers,)), dma((supers,)),
        dma((supers, 2, zs)), dma((supers, 2, zs)),
        dma((supers, 2, zs)), dma((supers, 2, zs)),
        dma((supers, 2, zs)), dma((supers, 2, zs)),
        dma((supers, 2, zs)), dma((supers, 2, zs)),
        dma((supers, 2, zs)), dma((supers, 2, zs)),
        dma((supers, 2)), dma((supers, 2)),
    ]
    return pl.pallas_call(
        functools.partial(kernel, n_rows, n_cols, x_his),
        out_shape=(
            pltpu.VMEM((supers, BS, width), F32),
            pltpu.VMEM((supers, width, width), F32),
        ),
        in_specs=[pl.BlockSpec(memory_space=pl.ANY), pl.BlockSpec(memory_space=pl.ANY), smem, smem],
        out_specs=(vmem, vmem),
        scratch_shapes=scratch,
        compiler_params=pltpu.CompilerParams(
            collective_id=0, has_side_effects=True, vmem_limit_bytes=60 * 2**20
        ),
    )(blocks, slices, *lists)


def solution(mesh):
    n_rows, n_cols = mesh.shape["row"], mesh.shape["col"]
    return jax.shard_map(
        functools.partial(local, n_rows, n_cols),
        mesh=mesh,
        in_specs=(P("row", "col"), P(None, "col", None), P(), P()),
        out_specs=(P(None, ("row", "col"), None), P()),
        check_vma=False,
    )
```

```python
import functools

import jax
import jax.numpy as jnp
from jax import lax
from jax.experimental import pallas as pl
from jax.experimental.pallas import tpu as pltpu
from jax.sharding import PartitionSpec as P

BS = 128
MESH = pl.DeviceIdType.MESH
F32 = jnp.float32
BF16 = jnp.bfloat16


def tables(block_slot, list_ids, n_rows, n_cols):
    n_blocks, listed = block_slot.shape[0], list_ids.shape[1]
    ids = jnp.arange(n_blocks, dtype=jnp.int32)
    slots = jnp.sum(jnp.where(list_ids[..., None] == ids, block_slot, 0), axis=-1)
    col_blocks, row_blocks = n_blocks // n_cols, n_blocks // n_rows
    row = slots // row_blocks
    pos = jnp.arange(listed, dtype=jnp.int32)
    before = pos[None, :] < pos[:, None]
    kth = jnp.sum(((row[:, :, None] == row[:, None, :]) & before).astype(jnp.int32), axis=-1)
    key = row * n_cols + kth
    keys = jnp.arange(n_rows * n_cols, dtype=jnp.int32)
    code = jnp.sum(jnp.where(key[:, None, :] == keys[:, None], (1 + slots * listed + pos)[:, None, :], 0), axis=-1)
    slot, place = jnp.maximum(code - 1, 0) // listed, jnp.maximum(code - 1, 0) % listed
    shard = listed // n_cols
    table = jnp.stack(
        [
            (code > 0).astype(jnp.int32), place // shard, slot // col_blocks, slot % col_blocks, slot % row_blocks,
            slot // col_blocks % 2,
        ]
    )
    return slots // col_blocks, table


SCALE_ROWS = 16
TOP = 32000.0


def encode(ref, block):
    top = jnp.max(jnp.abs(block), axis=0, keepdims=True)
    exponent = jnp.floor(jnp.log2(jnp.maximum(top, 1e-30))) + 1.0
    coded = jnp.floor(block * (jnp.exp2(-exponent) * TOP) + 0.5)
    ref[0:BS] = coded.astype(jnp.int32).astype(jnp.int16)
    exponents = jnp.broadcast_to(exponent, (SCALE_ROWS, block.shape[1]))
    ref[BS : BS + SCALE_ROWS] = exponents.astype(jnp.int32).astype(jnp.int16)


def decode(ref):
    exponent = ref[BS : BS + SCALE_ROWS].astype(jnp.int32).astype(F32)[0:1]
    return ref[0:BS].astype(jnp.int32).astype(F32) * (jnp.exp2(exponent) * (1.0 / TOP))


def kernel(
    n_rows, n_cols, x_his,
    inv_hbm, pan_hbm, cols, by_k,
    out, diag,
    pan, a_all, a_pick, p_send, p_recv_0, p_recv_1, p_all, l_recv, left,
    part, core_recv, z_send, z_recv, x_send, x_recv, d_part, d_sib, u_send, u_recv, v_send, v_recv, t_all,
    pan_sem, a_sem, p_ss, p_rs, b_ss, b_rs, ag_ss, ag_rs, as_ss, as_rs, l_ss, l_rs, m_ss, m_rs, c_ss, c_rs, z_ss, z_rs, x_ss, x_rs,
    ds_ss, ds_rs, u_ss, u_rs, v_ss, v_rs, t_ss, t_rs, w_ss, w_rs, er_ss, er_rs, es_ss, es_rs,
):
    supers = pan.shape[0]
    p_recv = (p_recv_0, p_recv_1)
    sub = BS // n_rows
    col_blocks = a_all.shape[0]
    shard = pan.shape[1]
    width = pan.shape[3]
    chips = n_cols // 2
    zs = chips // x_his
    ys = n_rows // 2
    me_r, me_c = lax.axis_index("row"), lax.axis_index("col")
    core = lax.rem(me_c, 2)
    chip = me_c // 2
    x_hi, z = chip // zs, lax.rem(chip, zs)
    sibling = (me_r, me_c + 1 - 2 * core)

    def remote(src, dst, ss, rs, to):
        return pltpu.make_async_remote_copy(
            src_ref=src, dst_ref=dst, send_sem=ss, recv_sem=rs, device_id=to, device_id_type=MESH
        )

    barrier = pltpu.get_barrier_semaphore()

    @pl.loop(1, n_cols)
    def _(d):
        pl.semaphore_signal(barrier, inc=1, device_id=(me_r, lax.rem(me_c + d, n_cols)), device_id_type=MESH)

    @pl.loop(1, n_rows)
    def _(d):
        pl.semaphore_signal(barrier, inc=1, device_id=(lax.rem(me_r + d, n_rows), me_c), device_id_type=MESH)

    opposite = (lax.rem(me_r + ys, n_rows), lax.rem(me_c + zs * 2, n_cols))
    pl.semaphore_signal(barrier, inc=1, device_id=opposite, device_id_type=MESH)

    load_pan = pltpu.make_async_copy(pan_hbm.at[:, :, me_r], pan, pan_sem)
    load_pan.start()

    def load_a(b):
        columns = pl.ds(pl.multiple_of(b * BS, BS), BS)
        return pltpu.make_async_copy(inv_hbm.at[:, :, columns], a_all.at[b], a_sem.at[b])

    @pl.loop(0, col_blocks)
    def _(b):
        load_a(b).start()

    load_pan.wait()

    def pick_for(c, s):
        piece = jnp.zeros((sub, width), BF16)
        for q in range(shard):
            piece = jnp.where(cols[s, me_c * shard + q] == c, pan[s, q], piece)
        return piece

    @pl.loop(1, n_cols)
    def _(d):
        for s in range(supers):
            p_send[s, d] = pick_for(lax.rem(me_c + d, n_cols), s)

    for s in range(supers):
        p_recv[s][core, me_c] = pick_for(me_c, s)

    pl.semaphore_wait(barrier, n_cols + n_rows - 1)

    def p_copy(s, d, source):
        to = (me_r, lax.rem(me_c + d, n_cols))
        return remote(p_send.at[s, d], p_recv[s].at[lax.rem(to[1], 2), source], p_ss.at[s, d], p_rs.at[s, d], to)

    for s in range(supers):
        @pl.loop(1, n_cols)
        def _(d, s=s):
            p_copy(s, d, me_c).start()

    def picks(s):
        @pl.loop(0, n_cols)
        def _(i):
            half_of, place = i // chips, lax.rem(i, chips)
            k = 2 * place + jnp.where(half_of == 1, core, 1 - core)
            a_row = by_k[4, s, me_r * n_cols + k]
            rows = pl.ds(pl.multiple_of(i * BS, BS), BS)
            for b in range(n_cols):
                block = a_all[by_k[3, s, chip * n_cols + b], a_row]
                here = by_k[0, s, chip * n_cols + b] * (by_k[2, s, chip * n_cols + b] == me_c) == 1
                a_pick[s, rows, b * BS : (b + 1) * BS] = jnp.where(here, block, jnp.zeros_like(block))

    @pl.loop(0, col_blocks)
    def _(b):
        load_a(b).wait()

    picks(0)

    def b_copy(s, of):
        return remote(p_recv[s].at[of], p_recv[s].at[of], b_ss.at[s], b_rs.at[s], sibling)

    def to_cores(s):
        @pl.loop(1, n_cols)
        def _(d):
            source = lax.rem(me_c - d + n_cols, n_cols)
            remote(p_send.at[s, d], p_recv[s].at[core, source], p_ss.at[s, d], p_rs.at[s, d], sibling).wait_recv()

        b_copy(s, core).start()

    mine = pl.ds(core * chips, chips)
    x_lo, y = me_r // ys, lax.rem(me_r, ys)
    up, down, across = x_lo * ys + lax.rem(y + 1, ys), x_lo * ys + lax.rem(y + ys - 1, ys), (1 - x_lo) * ys + y
    far = x_lo * ys + lax.rem(y + 2, ys)
    far_up, far_down = lax.rem(up + ys, n_rows), lax.rem(down + ys, n_rows)
    far_far = lax.rem(far + ys, n_rows)
    first = pl.ds(core * chips, chips // 2)
    second = pl.ds(core * chips + chips // 2, chips // 2)

    def ag_copy(s, j, slots, source, to):
        block = p_all.at[s, slots, source]
        return remote(block, block, ag_ss.at[s, j], ag_rs.at[s, j], (to, me_c))

    sends = {
        0: (mine, me_r, up), 1: (mine, me_r, down), 2: (mine, me_r, across),
        3: (first, down, up), 4: (second, up, down), 5: (mine, across, up), 6: (mine, across, down), 7: (mine, far, across),
    }
    arrivals = {
        0: (mine, down), 1: (mine, up), 2: (mine, across),
        3: (first, far), 4: (second, far), 5: (mine, far_down), 6: (mine, far_up), 7: (mine, far_far),
    }

    def ag_start(s, j):
        ag_copy(s, j, *sends[j]).start()

    def ag_wait(s, j):
        ag_copy(s, j, *arrivals[j], across).wait_recv()

    def as_copy(s, source, of):
        block = p_all.at[s, pl.ds(of * chips, chips), source]
        return remote(block, block, as_ss.at[s, source], as_rs.at[s, source], sibling)

    def pack(s):
        b_copy(s, 1 - core).wait_recv()
        for t in range(chips):
            k = core * chips + t
            block = p_recv[s][by_k[5, s, chip * n_cols + k], by_k[1, s, chip * n_cols + k]]
            valid = by_k[0, s, chip * n_cols + k] == 1
            p_all[s, k, me_r] = jnp.where(valid, block, jnp.zeros_like(block))

    def ag_first(s):
        for j in (0, 1, 2):
            ag_start(s, j)
        as_copy(s, me_r, core).start()

    def ag_second(s):
        ag_wait(s, 2)
        ag_start(s, 5)
        ag_start(s, 6)
        ag_wait(s, 0)
        ag_start(s, 3)
        ag_wait(s, 1)
        ag_start(s, 4)
        for source in (across, down, up):
            as_copy(s, source, core).start()

    def ag_third(s):
        ag_wait(s, 3)
        ag_wait(s, 4)
        ag_start(s, 7)
        ag_wait(s, 5)
        ag_wait(s, 6)
        for source in (far, far_down, far_up):
            as_copy(s, source, core).start()
        ag_wait(s, 7)
        as_copy(s, far_far, core).start()

    def l_copy(t):
        k = core * chips + t
        return remote(p_all.at[:, k, me_r], l_recv.at[chip], l_ss.at[t], l_rs.at[chip], (me_r, k))

    def l_arrive(j):
        return remote(p_all.at[:, 0, me_r], l_recv.at[j], l_ss.at[0], l_rs.at[j], sibling)

    def l_first():
        @pl.loop(0, chips)
        def _(t):
            k = core * chips + t

            @pl.when(k != me_c)
            def _():
                l_copy(t).start()

            @pl.when(k == me_c)
            def _():
                l_recv[chip] = p_all[:, k, me_r]

    def m_copy(d):
        g = lax.rem(me_r + d, n_rows)
        return remote(l_recv.at[g], left.at[:, me_r], m_ss.at[d], m_rs.at[d], (g, me_c))

    def m_arrive(d):
        source = lax.rem(me_r - d + n_rows, n_rows)
        return remote(l_recv.at[0], left.at[:, source], m_ss.at[d], m_rs.at[d], (source, me_c))

    def l_second():
        @pl.loop(0, chips)
        def _(j):
            @pl.when(2 * j + me_c // chips != me_c)
            def _():
                l_arrive(j).wait_recv()

        left[:, me_r] = l_recv[me_r]

        @pl.loop(1, n_rows)
        def _(d):
            m_copy(d).start()

    to_cores(0)
    pack(0)
    ag_first(0)
    picks(1)
    to_cores(1)
    ag_second(0)
    pack(1)
    ag_first(1)
    l_first()
    ag_third(0)
    ag_second(1)

    def c_copy(s, h):
        return remote(part.at[s, 0, h], core_recv.at[s, h], c_ss.at[s, h], c_rs.at[s, h], sibling)

    def z_copy(s, h, d):
        to = (me_r, (x_hi * zs + lax.rem(z + d, zs)) * 2 + core)
        return remote(z_send.at[s, h, d - 1], z_recv.at[s, h, d - 1], z_ss.at[s, h, d], z_rs.at[s, h, d], to)

    def products(s):
        @pl.loop(0, n_rows)
        def _(source):
            as_copy(s, source, 1 - core).wait_recv()

        def product(half_of, h):
            rows = pl.ds(pl.multiple_of((half_of * chips + h * zs) * BS, BS), zs * BS)
            result = jnp.dot(a_pick[s, rows, :], p_all[s].reshape(n_cols * BS, width), preferred_element_type=F32)
            part[s, half_of, h] = result.reshape(zs, BS, width)

        def to_z(h):
            c_copy(s, h).wait_recv()

            @pl.loop(1, zs)
            def _(d):
                there = lax.rem(z + d, zs)
                encode(z_send.at[s, h, d - 1], part[s, 1, h, there] + core_recv[s, h, there])
                z_copy(s, h, d).start()

        @pl.loop(0, x_his)
        def _(step):
            h = jnp.where(step == 0, 1 - x_hi, x_hi)
            product(0, h)
            c_copy(s, h).start()

            @pl.when(step > 0)
            def _():
                to_z(1 - x_hi)

            product(1, h)

        to_z(x_hi)

    products(0)
    ag_third(1)
    l_second()
    products(1)

    @pl.loop(1, n_rows)
    def _(d):
        m_arrive(d).wait_recv()

    def x_copy(s):
        to = (me_r, ((1 - x_hi) * zs + z) * 2 + core)
        return remote(x_send.at[s], x_recv.at[s], x_ss.at[s], x_rs.at[s], to)

    def over_z(s, h):
        total = part[s, 1, h, z] + core_recv[s, h, z]
        for d in range(1, zs):
            z_copy(s, h, d).wait_recv()
            total = total + decode(z_recv.at[s, h, d - 1])
        return total

    def start_x(s):
        encode(x_send.at[s], over_z(s, 1 - x_hi))
        x_copy(s).start()

    half = width // 2
    ring = zs
    piece, bit = half // ring, half // ring // ring
    x_at = x_hi * 2 + x_lo

    def ds_copy(s):
        there = pl.ds(pl.multiple_of((1 - core) * half, half), half)
        return remote(d_part.at[s, there], d_sib.at[s], ds_ss.at[s], ds_rs.at[s], sibling)

    def place_in(f, step):
        return y if f == step else z

    def peer_at(f, step, d):
        if step == 2:
            peer = lax.rem(x_at + d, ring)
            return peer, (lax.rem(peer, 2) * ys + y, ((peer // 2) * zs + z) * 2 + core)
        peer = lax.rem(place_in(f, step) + d, ring)
        return peer, (x_lo * ys + peer, me_c) if f == step else (me_r, (x_hi * zs + peer) * 2 + core)

    def u_copy(s, f, d):
        peer, to = peer_at(f, 0, d)
        return remote(u_send.at[s, f, peer], u_recv.at[s, f, d], u_ss.at[s, f, d], u_rs.at[s, f, d], to)

    def v_copy(s, f, d):
        peer, to = peer_at(f, 1, d)
        return remote(v_send.at[s, f, peer], v_recv.at[s, f, d], v_ss.at[s, f, d], v_rs.at[s, f, d], to)

    def t_copy(s, f, d, source):
        block = t_all.at[s, f, source]
        return remote(block, block, t_ss.at[s, f, d], t_rs.at[s, f, d], peer_at(f, 2, d)[1])

    def block_of(s, f, first, rows):
        return diag.at[s, pl.ds(pl.multiple_of(first, rows), rows), f * half : (f + 1) * half]

    def w_copy(s, f, d, source):
        block = block_of(s, f, core * half + place_in(f, 0) * piece + source * bit, bit)
        return remote(block, block, w_ss.at[s, f, d], w_rs.at[s, f, d], peer_at(f, 1, d)[1])

    def er_copy(s, f, d, source):
        block = block_of(s, f, core * half + source * piece, piece)
        return remote(block, block, er_ss.at[s, f, d], er_rs.at[s, f, d], peer_at(f, 0, d)[1])

    def es_copy(s, f, of):
        block = block_of(s, f, of * half, half)
        return remote(block, block, es_ss.at[s, f], es_rs.at[s, f], sibling)

    def finish_sums(s):
        total = over_z(s, x_hi)
        x_copy(s).wait_recv()
        total = total + decode(x_recv.at[s])
        valid = by_k[0, s, me_r * n_cols + me_c] == 1
        total = jnp.where(valid, total, jnp.zeros_like(total))
        out[s] = total
        total = -total
        high = total.astype(BF16)
        low = (total - high.astype(F32)).astype(BF16)
        contract = functools.partial(
            lax.dot_general, dimension_numbers=(((0,), (0,)), ((), ())), preferred_element_type=F32
        )
        for of in (1 - core, core):
            columns = pl.ds(pl.multiple_of(of * half, half), half)
            block = left[s, :, :, columns].reshape(BS, half)
            d_part[s, columns] = contract(block, high) + contract(block, low)
            if of is not core:
                ds_copy(s).start()

    def over_cores(s):
        ds_copy(s).wait_recv()
        here = pl.ds(pl.multiple_of(core * half, half), half)
        total = (d_part[s, here] + d_sib[s]).reshape(ring, piece, width)
        for f in range(2):
            u_send[s, f] = total[:, :, f * half : (f + 1) * half]
            for d in range(1, ring):
                u_copy(s, f, d).start()

    def over_first(s):
        for f in range(2):
            total = u_send[s, f, place_in(f, 0)]
            for d in range(1, ring):
                u_copy(s, f, d).wait_recv()
                total = total + u_recv[s, f, d]
            v_send[s, f] = total.reshape(ring, bit, half)
            for d in range(1, ring):
                v_copy(s, f, d).start()

    def over_second(s):
        for f in range(2):
            total = v_send[s, f, place_in(f, 1)]
            for d in range(1, ring):
                v_copy(s, f, d).wait_recv()
                total = total + v_recv[s, f, d]
            t_all[s, f, x_at] = total
            for d in range(1, ring):
                t_copy(s, f, d, x_at).start()

    def over_third(s):
        for f in range(2):
            for d in range(1, ring):
                t_copy(s, f, d, lax.rem(x_at - d + ring, ring)).wait_recv()
            total = t_all[s, f, 0]
            for x in range(1, ring):
                total = total + t_all[s, f, x]
            first = core * half + place_in(f, 0) * piece + place_in(f, 1) * bit
            diag[s, pl.ds(pl.multiple_of(first, bit), bit), f * half : (f + 1) * half] = total
            for d in range(1, ring):
                w_copy(s, f, d, place_in(f, 1)).start()

    def back_second(s):
        for f in range(2):
            for d in range(1, ring):
                w_copy(s, f, d, lax.rem(place_in(f, 1) - d + ring, ring)).wait_recv()
            for d in range(1, ring):
                er_copy(s, f, d, place_in(f, 0)).start()

    def back_first(s):
        for f in range(2):
            for d in range(1, ring):
                er_copy(s, f, d, lax.rem(place_in(f, 0) - d + ring, ring)).wait_recv()
            es_copy(s, f, core).start()

    start_x(0)
    finish_sums(0)
    start_x(1)
    over_cores(0)
    over_first(0)
    finish_sums(1)
    over_second(0)
    over_cores(1)
    over_third(0)
    over_first(1)
    back_second(0)
    over_second(1)
    back_first(0)
    over_third(1)
    back_second(1)
    back_first(1)

    for s in range(supers):
        @pl.loop(1, n_cols)
        def _(d, s=s):
            p_copy(s, d, me_c).wait_send()

        b_copy(s, core).wait_send()

    @pl.loop(0, chips)
    def _(t):
        @pl.when(core * chips + t != me_c)
        def _():
            l_copy(t).wait_send()

    @pl.loop(1, n_rows)
    def _(d):
        m_copy(d).wait_send()

    for s in range(supers):
        for j in sends:
            ag_copy(s, j, *sends[j]).wait_send()

        @pl.loop(0, n_rows)
        def _(source, s=s):
            as_copy(s, source, core).wait_send()

        for f in range(2):
            for d in range(1, ring):
                u_copy(s, f, d).wait_send()
                v_copy(s, f, d).wait_send()
                t_copy(s, f, d, x_at).wait_send()
                w_copy(s, f, d, place_in(f, 1)).wait_send()
                er_copy(s, f, d, place_in(f, 0)).wait_send()

            es_copy(s, f, core).wait_send()
            es_copy(s, f, 1 - core).wait_recv()

        for h in range(x_his):
            c_copy(s, h).wait_send()
            for d in range(1, zs):
                z_copy(s, h, d).wait_send()
        x_copy(s).wait_send()
        ds_copy(s).wait_send()


def local(n_rows, n_cols, inverse, panels, block_slot, list_ids):
    supers, _, width = panels.shape
    col_blocks = inverse.shape[1] // BS
    sub = BS // n_rows
    x_his = 2
    chips = n_cols // 2
    zs = chips // x_his
    half = width // 2
    lists = tables(block_slot, list_ids, n_rows, n_cols)
    blocks = inverse.reshape(-1, BS, inverse.shape[1])
    slices = panels.reshape(supers, -1, n_rows, sub, width)
    vmem = pl.BlockSpec(memory_space=pltpu.VMEM)
    smem = pl.BlockSpec(memory_space=pltpu.SMEM)
    dma = pltpu.SemaphoreType.DMA
    scratch = [
        pltpu.VMEM((supers, slices.shape[1], sub, width), BF16),
        pltpu.VMEM((col_blocks, blocks.shape[0], BS, BS), BF16),
        pltpu.VMEM((supers, n_cols * BS, n_cols * BS), BF16),
        pltpu.VMEM((supers, n_cols, sub, width), BF16),
        pltpu.VMEM((2, n_cols, sub, width), BF16),
        pltpu.VMEM((2, n_cols, sub, width), BF16),
        pltpu.VMEM((supers, n_cols, n_rows, sub, width), BF16),
        pltpu.VMEM((chips, supers, sub, width), BF16),
        pltpu.VMEM((supers, n_rows, sub, width), BF16),
        pltpu.VMEM((supers, 2, x_his, zs, BS, width), F32),
        pltpu.VMEM((supers, x_his, zs, BS, width), F32),
        pltpu.VMEM((supers, x_his, zs - 1, BS + SCALE_ROWS, width), jnp.int16),
        pltpu.VMEM((supers, x_his, zs - 1, BS + SCALE_ROWS, width), jnp.int16),
        pltpu.VMEM((supers, BS + SCALE_ROWS, width), jnp.int16),
        pltpu.VMEM((supers, BS + SCALE_ROWS, width), jnp.int16),
        pltpu.VMEM((supers, width, width), F32),
        pltpu.VMEM((supers, half, width), F32),
        pltpu.VMEM((supers, 2, zs, half // zs, half), F32),
        pltpu.VMEM((supers, 2, zs, half // zs, half), F32),
        pltpu.VMEM((supers, 2, zs, half // zs // zs, half), F32),
        pltpu.VMEM((supers, 2, zs, half // zs // zs, half), F32),
        pltpu.VMEM((supers, 2, zs, half // zs // zs, half), F32),
        dma(()),
        dma((col_blocks,)),
        dma((supers, n_cols)), dma((supers, n_cols)),
        dma((supers,)), dma((supers,)),
        dma((supers, 8)), dma((supers, 8)),
        dma((supers, n_rows)), dma((supers, n_rows)),
        dma((chips,)), dma((chips,)),
        dma((n_rows,)), dma((n_rows,)),
        dma((supers, x_his)), dma((supers, x_his)),
        dma((supers, x_his, zs)), dma((supers, x_his, zs)),
        dma((supers,)), dma((supers,)),
        dma((supers,)), dma((supers,)),
        dma((supers, 2, zs)), dma((supers, 2, zs)),
        dma((supers, 2, zs)), dma((supers, 2, zs)),
        dma((supers, 2, zs)), dma((supers, 2, zs)),
        dma((supers, 2, zs)), dma((supers, 2, zs)),
        dma((supers, 2, zs)), dma((supers, 2, zs)),
        dma((supers, 2)), dma((supers, 2)),
    ]
    return pl.pallas_call(
        functools.partial(kernel, n_rows, n_cols, x_his),
        out_shape=(
            pltpu.VMEM((supers, BS, width), F32),
            pltpu.VMEM((supers, width, width), F32),
        ),
        in_specs=[pl.BlockSpec(memory_space=pl.ANY), pl.BlockSpec(memory_space=pl.ANY), smem, smem],
        out_specs=(vmem, vmem),
        scratch_shapes=scratch,
        compiler_params=pltpu.CompilerParams(
            collective_id=0, has_side_effects=True, vmem_limit_bytes=60 * 2**20
        ),
    )(blocks, slices, *lists)


def solution(mesh):
    n_rows, n_cols = mesh.shape["row"], mesh.shape["col"]
    return jax.shard_map(
        functools.partial(local, n_rows, n_cols),
        mesh=mesh,
        in_specs=(P("row", "col"), P(None, "col", None), P(), P()),
        out_specs=(P(None, ("row", "col"), None), P()),
        check_vma=False,
    )
```
